512 devices in a mesh: pix: 16 (over z, core), frm: 32 (over y, x).
Axes of the slice: x: 4, y: 8, z: 8, core: 2. Of those that a mesh axis runs over, the one named last changes fastest.
Arguments:
- video: bfloat16 [16384, 8192], P('pix', 'frm'), may hold values from -6 to 6
- sparse: float32 [16384, 8192], P('pix', 'frm'), may hold values from -4 to 4
- multiplier: float32 [16384, 8192], P('pix', 'frm'), may hold values from -3 to 3
- start_block: bfloat16 [8192, 64], P('frm'), may hold values from -6 to 6
Outputs:
- sparse_next: float32 [16384, 8192], P('pix', 'frm')
- multiplier_next: float32 [16384, 8192], P('pix', 'frm')
- residual_ratio: float32 [8192], P('frm')
The draws below stay inside these ranges and needn't reach their ends.
All inputs are finite; a program needn't handle non-finite values.
Results may differ from the reference program's by a relative error of at most 0.03.
Values may be sent and summed in bfloat16 or wider, within the bound.
No kernel may reach another device: no remote copies, remote signals or barrier semaphores. Data moves between devices by JAX's collectives and lax.ppermute only.
A program may use at most 64 MiB of HBM per device.

```python
import jax
import jax.numpy as jnp
from jax import lax

FR_DEV = 256
BLOCK = 64
PIXELS = 16384
FRAMES = 8192
N_FRM = 32


def background_draw(key, scale_lo, scale_hi, row_top):
    row_key, col_key, size_key = jax.random.split(key, 3)
    row_factor = jax.random.normal(row_key, (PIXELS, BLOCK), jnp.float32)
    col_factor = jax.random.normal(col_key, (FRAMES, BLOCK), jnp.float32)
    levels = jnp.exp(jax.random.uniform(size_key, (BLOCK,), jnp.float32, jnp.log(scale_lo), jnp.log(scale_hi)))
    position = jnp.arange(PIXELS, dtype=jnp.float32) / (PIXELS - 1.0)
    row_scale = jnp.exp(position * jnp.log(row_top))
    scaled = row_factor * (levels / jnp.sqrt(1.0 * BLOCK)) * row_scale[:, None]
    return jnp.dot(scaled, col_factor.T, precision=lax.Precision.HIGHEST)


def draw_video(key, part):
    key = jax.random.fold_in(key, 11)
    base_key, noise_key = jax.random.split(key)
    background = background_draw(base_key, 0.25, 0.8, 5.0)
    noise = 0.3 * jax.random.normal(noise_key, (PIXELS, FRAMES), jnp.float32)
    return jnp.clip(background + noise, -6.0, 6.0).astype(jnp.bfloat16)


def level_of(key, dims, shards, least, high):
    loudness = 1.0
    for axis_at, blocks in shards:
        heights = jax.random.uniform(jax.random.fold_in(jax.random.fold_in(key, 6), axis_at), (blocks,), jnp.float32, least / len(shards), high / len(shards))
        loudness = loudness * jnp.repeat(jnp.exp(heights), dims[axis_at] // blocks).reshape((-1,) + (1,) * (len(dims) - 1 - axis_at))
    return loudness


def scatter_about(own_key, extent, spread, reach, pieces=(), held_as=jnp.bfloat16):
    factor_of = level_of(own_key, extent, pieces, -0.22, 0.18) if pieces else 1.0
    result = jax.random.normal(own_key, extent, jnp.float32) * spread * factor_of
    return jnp.minimum(jnp.maximum(result, -reach), reach).astype(held_as)


def setup_inputs(seed: int = 0) -> dict:
    seeds = jax.random.split(jax.random.key(seed), 5)
    video = draw_video(jax.random.fold_in(seeds[4], 71), 0)
    sparse = scatter_about(seeds[1], (PIXELS, FRAMES), 0.5, 4.0, ((0, 16), (1, 32)), jnp.float32)
    multiplier = scatter_about(seeds[2], (PIXELS, FRAMES), 0.4, 3.0, ((0, 16), (1, 32)), jnp.float32)
    start_block = scatter_about(seeds[3], (FRAMES, BLOCK), 1.0, 6.0, ((0, 32),))
    return {"video": video, "sparse": sparse, "multiplier": multiplier, "start_block": start_block}


mu_value = 1.25
sparse_cut = 0.8
shrink_ratio = 0.25
epsilon_value = 1e-06

def reference(video, sparse, multiplier, start_block):
    highest = lax.Precision.HIGHEST
    video_full = video.astype(jnp.float32)
    working = (video_full - sparse + multiplier / mu_value).astype(jnp.bfloat16)
    working_groups = working.reshape(PIXELS, N_FRM, FR_DEV).astype(jnp.float32)
    start_groups = start_block.reshape(N_FRM, FR_DEV, BLOCK).astype(jnp.float32)
    partial_rows = jnp.einsum('pnf,nfb->npb', working_groups, start_groups)
    partial_half = lax.optimization_barrier(partial_rows.astype(jnp.bfloat16))
    across = lax.optimization_barrier(jnp.sum(partial_half.astype(jnp.float32), axis=0)).astype(jnp.bfloat16)
    krylov = lax.dot_general(working.astype(jnp.float32), across.astype(jnp.float32), (((0,), (0,)), ((), ())), preferred_element_type=jnp.float32)
    gram_block = jnp.dot(krylov.T, krylov, precision=highest)
    factor = jnp.linalg.cholesky(gram_block)
    subspace = jax.scipy.linalg.solve_triangular(factor, krylov.T, lower=True).T
    subspace_half = subspace.astype(jnp.bfloat16)
    projected = jnp.dot(working.astype(jnp.float32), subspace_half.astype(jnp.float32), preferred_element_type=jnp.float32)
    projected_gram = jnp.dot(projected.T, projected, precision=highest)
    shrink_level = jnp.trace(projected_gram) * (shrink_ratio / BLOCK)
    shifted_gram = projected_gram + shrink_level * jnp.eye(BLOCK, dtype=jnp.float32)
    weights = jax.scipy.linalg.cho_solve((jnp.linalg.cholesky(shifted_gram), True), projected_gram)
    expanded = jnp.dot(subspace, weights.T, precision=highest)
    low_rank = jnp.dot(projected, expanded.T, precision=highest)
    shifted = video_full - low_rank + multiplier / mu_value
    sparse_next = jnp.sign(shifted) * jnp.maximum(jnp.abs(shifted) - sparse_cut, 0.0)
    residual = video_full - low_rank - sparse_next
    multiplier_next = multiplier + mu_value * residual
    residual_sq = lax.optimization_barrier(jnp.sum(residual * residual, axis=0))
    video_sq = lax.optimization_barrier(jnp.sum(video_full * video_full, axis=0))
    residual_ratio = jnp.sqrt(residual_sq / (video_sq + epsilon_value))
    return (sparse_next, multiplier_next, residual_ratio)
```

```python
import functools

import jax
import jax.numpy as jnp
from jax import lax
from jax.experimental import pallas as pl
from jax.experimental.pallas import tpu as pltpu
from jax.sharding import PartitionSpec as P

mu_value = 1.25
inverse_mu = 0.8
sparse_cut = 0.8
shrink_ratio = 0.25
epsilon_value = 1e-06

f32 = jnp.float32
bf16 = jnp.bfloat16
highest = lax.Precision.HIGHEST

FRM = 32
PIX = 16
ROWS = 1024
HALF = 512
COLS = 256
RANK = 64
STEPS = 4
TILE = HALF // STEPS
SLICE = HALF // FRM

vmem = pl.BlockSpec(memory_space=pltpu.VMEM)
params = pltpu.CompilerParams(vmem_limit_bytes=40 * 1024 * 1024)


def dot_nt(a, b, **kw):
    return lax.dot_general(a, b, (((1,), (1,)), ((), ())), preferred_element_type=f32, **kw)


def dot_tn(a, b, **kw):
    return lax.dot_general(a, b, (((0,), (0,)), ((), ())), preferred_element_type=f32, **kw)


def dot_nn(a, b, **kw):
    return lax.dot_general(a, b, (((1,), (0,)), ((), ())), preferred_element_type=f32, **kw)


def split_two(x):
    hi = x.astype(bf16)
    return hi, (x - hi.astype(f32)).astype(bf16)


def split_three(x):
    hi = x.astype(bf16)
    rest = x - hi.astype(f32)
    mid = rest.astype(bf16)
    return hi, mid, (rest - mid.astype(f32)).astype(bf16)


def sub_iota():
    return lax.broadcasted_iota(jnp.int32, (8, 128), 0)


def lane_iota():
    return lax.broadcasted_iota(jnp.int32, (8, 128), 1)


def row_of(x, k):
    return jnp.broadcast_to(x[k : k + 1, :], (8, 128))


def column_of(x, c):
    return jnp.broadcast_to(x[:, c : c + 1], (8, 128))


def augment(a):
    blocks = []
    for b in range(8):
        eye = jnp.where(lane_iota() == sub_iota() + (8 * b + 64), 1.0, 0.0).astype(f32)
        part = a[8 * b : 8 * b + 8]
        blocks.append(jnp.where(lane_iota() < 64, jnp.concatenate([part, part], axis=1), eye))
    return blocks


def eliminate(blocks, factor):
    sub = sub_iota()
    rows = []
    for b in range(8):
        lead = blocks[b]
        cols = [column_of(lead, 8 * b + j) for j in range(8)]
        for k in range(8):
            at = sub == k
            pivot_row, pivot = row_of(lead, k), row_of(cols[k], k)
            if factor:
                root = lax.rsqrt(pivot)
                rows.append(pivot_row * root)
                inverse = root * root
            else:
                inverse = 1.0 / pivot
            scaled = pivot_row * inverse
            mult = cols[k]
            lead = jnp.where(at, scaled, lead - mult * scaled)
            for j in range(k + 1, 8):
                entry = row_of(cols[j], k) * inverse
                cols[j] = jnp.where(at, entry, cols[j] - mult * entry)
        blocks[b] = lead
        lead_rows = [row_of(lead, j) for j in range(8)]
        for i in range(b + 1 if factor else 0, 8):
            if i == b:
                continue
            block = blocks[i]
            total = block
            for j in range(8):
                total = total - column_of(block, 8 * b + j) * lead_rows[j]
            blocks[i] = total
    return rows if factor else blocks


def start_kernel(video, sparse, multiplier, start, working, across):
    start_block = start[...]
    halves = []
    for h in range(2):
        value = video[h].astype(f32) - sparse[h] + multiplier[h] * inverse_mu
        value = value.astype(bf16)
        working[h] = value
        halves.append(dot_nn(value, start_block))
    across[...] = jnp.concatenate(halves, axis=1).astype(bf16)


def sum_kernel(peers, x, out):
    total = x[0].astype(f32)
    for i in range(1, x.shape[0]):
        total = total + x[i].astype(f32)
    total = total.astype(out.dtype)
    for i in range(peers):
        out[i] = total


def krylov_kernel(across, working, out):
    packed = across[...].reshape(HALF, 128)
    first = dot_tn(packed, working[0])
    second = dot_tn(packed, working[1])
    krylov = first[:RANK] + second[RANK:]
    for i in range(8):
        out[i] = krylov[8 * i : 8 * i + 8, :128]
        out[8 + i] = krylov[8 * i : 8 * i + 8, 128:]


def project_kernel(gathered, working, krylov_out, out):
    packed = gathered[...].reshape(128, 128)
    krylov = jnp.concatenate([packed[:RANK], packed[RANK:]], axis=1)
    krylov_out[...] = krylov
    zero = jnp.zeros((RANK, COLS), bf16)
    total = None
    for part in reversed(split_three(krylov)):
        low = dot_nt(working[0], jnp.concatenate([part, zero], axis=0))
        high = dot_nt(working[1], jnp.concatenate([zero, part], axis=0))
        total = low + high if total is None else total + (low + high)
    gram = dot_nt(krylov, krylov, precision=highest)
    gram = jnp.concatenate([gram[:32], gram[32:]], axis=1)
    blank = jnp.zeros((7, 128), f32)
    for i in range(FRM):
        out[i, :SLICE] = total[SLICE * i : SLICE * i + SLICE]
        out[i, SLICE:] = jnp.concatenate([gram[i : i + 1], blank], axis=0)


def basis_kernel(gathered, krylov, projected_out, subspace_out, out, rows_ref):
    gram = jnp.concatenate([gathered[i, SLICE : SLICE + 1] for i in range(FRM)], axis=0)
    gram = jnp.concatenate([gram[:, :RANK], gram[:, RANK:]], axis=0)
    for i, row in enumerate(eliminate(augment(gram), True)):
        rows_ref[i : i + 1] = row[0:1]
    inverse = rows_ref[:, RANK:]
    zero = jnp.zeros((RANK, RANK), f32)
    pair = jnp.concatenate(
        [jnp.concatenate([inverse, zero], axis=1), jnp.concatenate([zero, inverse], axis=1)], axis=0
    )
    packed = gathered[:, :SLICE].reshape(HALF, 128)
    projected = dot_nt(packed, pair, precision=highest)
    projected_out[...] = projected
    subspace_out[...] = dot_nn(inverse, krylov[...], precision=highest)
    hi, lo = split_two(projected)
    gram = dot_tn(hi, hi) + (dot_tn(hi, lo) + dot_tn(lo, hi))
    gram = gram[:RANK, :RANK] + gram[RANK:, RANK:]
    gram = jnp.concatenate([gram[:32], gram[32:]], axis=1).astype(bf16)
    for i in range(PIX):
        out[i] = gram


def finish_kernel(grams, subspace, video, multiplier, projected, sparse_out, multiplier_out, out, weighted, sums):
    step = pl.program_id(0)

    @pl.when(step == 0)
    def _():
        gram = grams[0].astype(f32)
        for i in range(1, PIX):
            gram = gram + grams[i].astype(f32)
        gram = jnp.concatenate([gram[:, :RANK], gram[:, RANK:]], axis=0)
        rows = lax.broadcasted_iota(jnp.int32, (RANK, RANK), 0)
        cols = lax.broadcasted_iota(jnp.int32, (RANK, RANK), 1)
        eye = jnp.where(rows == cols, 1.0, 0.0).astype(f32)
        level = jnp.sum(jnp.sum(gram * eye, axis=0, keepdims=True), axis=1, keepdims=True) * (shrink_ratio / RANK)
        blocks = eliminate(augment(gram + level * eye), False)
        inverse = jnp.concatenate(blocks, axis=0)[:, RANK:]
        weights = eye - level * inverse
        mixed = dot_nn(weights, subspace[...], precision=highest)
        zero = jnp.zeros((RANK, COLS), bf16)
        for i, part in enumerate(split_two(mixed)):
            weighted[0, i] = jnp.concatenate([part, zero], axis=0)
            weighted[1, i] = jnp.concatenate([zero, part], axis=0)
        sums[...] = jnp.zeros_like(sums)

    hi, lo = split_two(projected[...])
    for h in range(2):
        low_rank = dot_nn(hi, weighted[h, 0]) + (dot_nn(hi, weighted[h, 1]) + dot_nn(lo, weighted[h, 0]))
        video_full = video[h].astype(f32)
        held = multiplier[h]
        base = video_full - low_rank
        shifted = base + held * inverse_mu
        sparse_next = shifted - jnp.clip(shifted, -sparse_cut, sparse_cut)
        residual = base - sparse_next
        sparse_out[h] = sparse_next
        multiplier_out[h] = held + mu_value * residual
        squares = (residual * residual).reshape(TILE // 8, 8, COLS)
        sums[0] += jnp.sum(squares, axis=0)
        squares = (video_full * video_full).reshape(TILE // 8, 8, COLS)
        sums[1] += jnp.sum(squares, axis=0)

    @pl.when(step == STEPS - 1)
    def _():
        residual_sq = jnp.sum(sums[0], axis=0, keepdims=True)
        video_sq = jnp.sum(sums[1], axis=0, keepdims=True)
        tile = jnp.concatenate(
            [residual_sq[:, :128], residual_sq[:, 128:], video_sq[:, :128], video_sq[:, 128:], jnp.zeros((4, 128), f32)],
            axis=0,
        )
        for i in range(PIX):
            out[i] = tile


def ratio_kernel(x, out):
    total = x[0]
    for i in range(1, PIX):
        total = total + x[i]
    out[...] = jnp.sqrt(total[0:2] / (total[2:4] + epsilon_value))


def struct(shape, dtype=f32):
    return jax.ShapeDtypeStruct(shape, dtype)


def whole(kernel, outs, count, **kw):
    return pl.pallas_call(
        kernel,
        out_shape=outs,
        in_specs=[vmem] * count,
        out_specs=jax.tree.map(lambda _: vmem, outs),
        compiler_params=params,
        **kw,
    )


def exchange(x, axis):
    return lax.all_to_all(x, axis, 0, 0)


def per_device(video, sparse, multiplier, start_block):
    video, sparse, multiplier = (x.reshape(2, HALF, COLS) for x in (video, sparse, multiplier))
    tall = pl.BlockSpec((2, TILE, COLS), lambda i: (0, i, 0))
    packed = pl.BlockSpec((TILE, 128), lambda i: (i, 0))

    working, across = pl.pallas_call(
        start_kernel,
        grid=(STEPS,),
        out_shape=(struct((2, HALF, COLS), bf16), struct((HALF, 128), bf16)),
        in_specs=[tall, tall, tall, pl.BlockSpec((COLS, RANK), lambda i: (0, 0))],
        out_specs=(tall, packed),
        compiler_params=params,
    )(video, sparse, multiplier, start_block)

    across = exchange(across.reshape(FRM, SLICE, 128), "frm")
    across = whole(functools.partial(sum_kernel, FRM), struct((FRM, SLICE, 128), bf16), 1)(across)
    across = exchange(across, "frm")

    krylov = whole(krylov_kernel, struct((PIX, 8, 128)), 2)(across, working)
    krylov = exchange(krylov, "pix")
    krylov = whole(functools.partial(sum_kernel, PIX), struct((PIX, 8, 128)), 1)(krylov)
    krylov = exchange(krylov, "pix")

    wide = struct((FRM, SLICE + 8, 128))
    krylov, projected = whole(project_kernel, (struct((RANK, COLS)), wide), 2)(krylov, working)
    projected = exchange(projected, "frm")
    projected = whole(functools.partial(sum_kernel, FRM), wide, 1)(projected)
    projected = exchange(projected, "frm")

    projected, subspace, grams = whole(
        basis_kernel,
        (struct((HALF, 128)), struct((RANK, COLS)), struct((PIX, 32, 128), bf16)),
        2,
        scratch_shapes=[pltpu.VMEM((RANK, 128), f32)],
    )(projected, krylov)
    grams = exchange(grams, "pix")

    sparse_next, multiplier_next, sums = pl.pallas_call(
        finish_kernel,
        grid=(STEPS,),
        out_shape=(struct((2, HALF, COLS)), struct((2, HALF, COLS)), struct((PIX, 8, 128))),
        in_specs=[
            pl.BlockSpec((PIX, 32, 128), lambda i: (0, 0, 0)),
            pl.BlockSpec((RANK, COLS), lambda i: (0, 0)),
            tall,
            tall,
            packed,
        ],
        out_specs=(tall, tall, pl.BlockSpec((PIX, 8, 128), lambda i: (0, 0, 0))),
        scratch_shapes=[pltpu.VMEM((2, 2, 128, COLS), bf16), pltpu.VMEM((2, 8, COLS), f32)],
        compiler_params=params,
    )(grams, subspace, video, multiplier, projected)
    sums = exchange(sums, "pix")
    ratio = whole(ratio_kernel, struct((2, 128)), 1)(sums)

    shape = (ROWS, COLS)
    return sparse_next.reshape(shape), multiplier_next.reshape(shape), ratio.reshape(COLS)


def solution(mesh):
    placed = (P("pix", "frm"), P("pix", "frm"), P("pix", "frm"), P("frm", None))
    return jax.shard_map(
        per_device,
        mesh=mesh,
        in_specs=placed,
        out_specs=(P("pix", "frm"), P("pix", "frm"), P("frm")),
        check_vma=False,
    )
```

```python
import functools

import jax
import jax.numpy as jnp
from jax import lax
from jax.experimental import pallas as pl
from jax.experimental.pallas import tpu as pltpu
from jax.sharding import PartitionSpec as P

mu_value = 1.25
inverse_mu = 0.8
sparse_cut = 0.8
shrink_ratio = 0.25
epsilon_value = 1e-06

f32 = jnp.float32
bf16 = jnp.bfloat16
highest = lax.Precision.HIGHEST

FRM = 32
PIX = 16
ROWS = 1024
HALF = 512
COLS = 256
RANK = 64
START_STEPS = 2
START_TILE = HALF // START_STEPS
STEPS = 4
TILE = HALF // STEPS
SLICE = HALF // FRM
CHUNK = SLICE + 1

vmem = pl.BlockSpec(memory_space=pltpu.VMEM)
params = pltpu.CompilerParams(vmem_limit_bytes=40 * 1024 * 1024)


def dot_nt(a, b, **kw):
    return lax.dot_general(a, b, (((1,), (1,)), ((), ())), preferred_element_type=f32, **kw)


def dot_tn(a, b, **kw):
    return lax.dot_general(a, b, (((0,), (0,)), ((), ())), preferred_element_type=f32, **kw)


def dot_nn(a, b, **kw):
    return lax.dot_general(a, b, (((1,), (0,)), ((), ())), preferred_element_type=f32, **kw)


def split_two(x):
    hi = x.astype(bf16)
    return hi, (x - hi.astype(f32)).astype(bf16)


def split_three(x):
    hi = x.astype(bf16)
    rest = x - hi.astype(f32)
    mid = rest.astype(bf16)
    return hi, mid, (rest - mid.astype(f32)).astype(bf16)


def sub_iota():
    return lax.broadcasted_iota(jnp.int32, (8, 128), 0)


def lane_iota():
    return lax.broadcasted_iota(jnp.int32, (8, 128), 1)


def row_of(x, k):
    return jnp.broadcast_to(x[k : k + 1, :], (8, 128))


def column_of(x, c):
    return jnp.broadcast_to(x[:, c : c + 1], (8, 128))


def augment(a):
    blocks = []
    for b in range(8):
        eye = jnp.where(lane_iota() == sub_iota() + (8 * b + 64), 1.0, 0.0).astype(f32)
        part = a[8 * b : 8 * b + 8]
        blocks.append(jnp.where(lane_iota() < 64, jnp.concatenate([part, part], axis=1), eye))
    return blocks


def eliminate(blocks, factor):
    sub = sub_iota()
    rows = []
    for b in range(8):
        lead = blocks[b]
        cols = [column_of(lead, 8 * b + j) for j in range(8)]
        for k in range(8):
            at = sub == k
            pivot_row, pivot = row_of(lead, k), row_of(cols[k], k)
            if factor:
                root = lax.rsqrt(pivot)
                rows.append(pivot_row * root)
                inverse = root * root
            else:
                inverse = 1.0 / pivot
            scaled = pivot_row * inverse
            mult = cols[k]
            lead = jnp.where(at, scaled, lead - mult * scaled)
            for j in range(k + 1, 8):
                entry = row_of(cols[j], k) * inverse
                cols[j] = jnp.where(at, entry, cols[j] - mult * entry)
        blocks[b] = lead
        lead_rows = [row_of(lead, j) for j in range(8)]
        for i in range(b + 1 if factor else 0, 8):
            if i == b:
                continue
            block = blocks[i]
            total = block
            for j in range(8):
                total = total - column_of(block, 8 * b + j) * lead_rows[j]
            blocks[i] = total
    return rows if factor else blocks


def start_kernel(video, sparse, multiplier, start, working, across, video_in, sparse_in, multiplier_in, start_in, sems):
    sources = ((video, video_in), (sparse, sparse_in), (multiplier, multiplier_in))
    copies = [pltpu.make_async_copy(start, start_in, sems.at[3 * START_STEPS])]
    for i in range(START_STEPS):
        rows = pl.ds(START_TILE * i, START_TILE)
        for j, (source, target) in enumerate(sources):
            copies.append(pltpu.make_async_copy(source.at[:, rows], target.at[:, rows], sems.at[3 * i + j]))
    for copy in copies:
        copy.start()
    copies[0].wait()
    for i in range(START_STEPS):
        rows = slice(START_TILE * i, START_TILE * i + START_TILE)
        for copy in copies[1 + 3 * i : 4 + 3 * i]:
            copy.wait()
        halves = []
        for h in range(2):
            value = video_in[h, rows].astype(f32) - sparse_in[h, rows] + multiplier_in[h, rows] * inverse_mu
            value = value.astype(bf16)
            working[h, rows] = value
            halves.append(dot_nt(value, start_in[...]))
        across[rows] = jnp.concatenate(halves, axis=1).astype(bf16)


def sum_kernel(peers, x, out):
    rows = x.shape[0] // peers
    total = x[:rows].astype(f32)
    for i in range(1, peers):
        total = total + x[rows * i : rows * i + rows].astype(f32)
    total = total.astype(out.dtype)
    for i in range(peers):
        out[rows * i : rows * i + rows] = total


def krylov_kernel(across, working, out):
    packed = across[...]
    first = dot_tn(packed, working[0])
    second = dot_tn(packed, working[1])
    krylov = first[:RANK] + second[RANK:]
    for i in range(8):
        out[8 * i : 8 * i + 8] = krylov[8 * i : 8 * i + 8, :128]
        out[RANK + 8 * i : RANK + 8 * i + 8] = krylov[8 * i : 8 * i + 8, 128:]


def project_kernel(gathered, working, krylov_out, out):
    packed = gathered[...]
    krylov = jnp.concatenate([packed[:RANK], packed[RANK:]], axis=1)
    krylov_out[...] = krylov
    zero = jnp.zeros((RANK, COLS), bf16)
    total = None
    for part in reversed(split_three(krylov)):
        low = dot_nt(working[0], jnp.concatenate([part, zero], axis=0))
        high = dot_nt(working[1], jnp.concatenate([zero, part], axis=0))
        total = low + high if total is None else total + (low + high)
    gram = dot_nt(krylov, krylov, precision=highest)
    gram = jnp.concatenate([gram[:32], gram[32:]], axis=1)
    for i in range(FRM):
        at = CHUNK * i
        out[at : at + SLICE] = total[SLICE * i : SLICE * i + SLICE]
        out[at + SLICE : at + CHUNK] = gram[i : i + 1]


def basis_kernel(gathered, krylov, projected_out, subspace_out, out, rows_ref):
    gram = jnp.concatenate([gathered[CHUNK * i + SLICE : CHUNK * i + CHUNK] for i in range(FRM)], axis=0)
    gram = jnp.concatenate([gram[:, :RANK], gram[:, RANK:]], axis=0)
    for i, row in enumerate(eliminate(augment(gram), True)):
        rows_ref[i : i + 1] = row[0:1]
    inverse = rows_ref[:, RANK:]
    zero = jnp.zeros((RANK, RANK), f32)
    pair = jnp.concatenate(
        [jnp.concatenate([inverse, zero], axis=1), jnp.concatenate([zero, inverse], axis=1)], axis=0
    )
    packed = jnp.concatenate([gathered[CHUNK * i : CHUNK * i + SLICE] for i in range(FRM)], axis=0)
    projected = dot_nt(packed, pair, precision=highest)
    projected_out[...] = projected
    subspace_out[...] = dot_nn(inverse, krylov[...], precision=highest)
    hi, lo = split_two(projected)
    gram = dot_tn(hi, hi) + (dot_tn(hi, lo) + dot_tn(lo, hi))
    gram = gram[:RANK, :RANK] + gram[RANK:, RANK:]
    gram = jnp.concatenate([gram[:32], gram[32:]], axis=1).astype(bf16)
    for i in range(PIX):
        out[32 * i : 32 * i + 32] = gram


def finish_kernel(grams, subspace, video, multiplier, projected, sparse_out, multiplier_out, out, near, sems):
    gram = grams[:32].astype(f32)
    for i in range(1, PIX):
        gram = gram + grams[32 * i : 32 * i + 32].astype(f32)
    gram = jnp.concatenate([gram[:, :RANK], gram[:, RANK:]], axis=0)
    rows = lax.broadcasted_iota(jnp.int32, (RANK, RANK), 0)
    cols = lax.broadcasted_iota(jnp.int32, (RANK, RANK), 1)
    eye = jnp.where(rows == cols, 1.0, 0.0).astype(f32)
    level = jnp.sum(jnp.sum(gram * eye, axis=0, keepdims=True), axis=1, keepdims=True) * (shrink_ratio / RANK)
    blocks = eliminate(augment(gram + level * eye), False)
    inverse = jnp.concatenate(blocks, axis=0)[:, RANK:]
    weights = eye - level * inverse
    mixed = dot_nn(weights, subspace[...], precision=highest)
    zero = jnp.zeros((RANK, COLS), bf16)
    parts = split_two(mixed)
    weighted = [[jnp.concatenate(pair, axis=0) for pair in ((part, zero), (zero, part))] for part in parts]

    residual_sq = jnp.zeros((8, COLS), f32)
    video_sq = jnp.zeros((8, COLS), f32)
    copies = []
    for i in range(STEPS):
        rows = slice(TILE * i, TILE * i + TILE)
        hi, lo = split_two(projected[rows])
        for h in range(2):
            low_rank = dot_nn(hi, weighted[0][h]) + (dot_nn(hi, weighted[1][h]) + dot_nn(lo, weighted[0][h]))
            video_full = video[h, rows].astype(f32)
            held = multiplier[h, rows]
            base = video_full - low_rank
            shifted = base + held * inverse_mu
            sparse_next = shifted - jnp.clip(shifted, -sparse_cut, sparse_cut)
            residual = base - sparse_next
            near[0, h, rows] = sparse_next
            near[1, h, rows] = held + mu_value * residual
            for j, target in enumerate((sparse_out, multiplier_out)):
                at = (h, pl.ds(TILE * i, TILE))
                copies.append(pltpu.make_async_copy(near.at[j].at[at], target.at[at], sems.at[len(copies)]))
                copies[-1].start()
            residual_sq += jnp.sum((residual * residual).reshape(TILE // 8, 8, COLS), axis=0)
            video_sq += jnp.sum((video_full * video_full).reshape(TILE // 8, 8, COLS), axis=0)
    residual_sq = jnp.sum(residual_sq, axis=0, keepdims=True)
    video_sq = jnp.sum(video_sq, axis=0, keepdims=True)
    tile = jnp.concatenate(
        [residual_sq[:, :128], residual_sq[:, 128:], video_sq[:, :128], video_sq[:, 128:], jnp.zeros((4, 128), f32)],
        axis=0,
    )
    for i in range(PIX):
        out[8 * i : 8 * i + 8] = tile
    for copy in copies:
        copy.wait()


def ratio_kernel(x, out):
    total = x[:8]
    for i in range(1, PIX):
        total = total + x[8 * i : 8 * i + 8]
    out[...] = jnp.sqrt(total[0:2] / (total[2:4] + epsilon_value))


def struct(shape, dtype=f32):
    return jax.ShapeDtypeStruct(shape, dtype)


def whole(kernel, outs, count, **kw):
    return pl.pallas_call(
        kernel,
        out_shape=outs,
        in_specs=[vmem] * count,
        out_specs=jax.tree.map(lambda _: vmem, outs),
        compiler_params=params,
        **kw,
    )


def exchange(x, axis):
    peers = FRM if axis == "frm" else PIX
    parts = (peers, 1, -1) if x.dtype == f32 else (peers, -1, 128)
    return lax.all_to_all(x.reshape(parts), axis, 0, 0).reshape(x.shape)


def per_device(video, sparse, multiplier, start_block):
    video, sparse, multiplier = (x.reshape(2, HALF, COLS) for x in (video, sparse, multiplier))
    far = pl.BlockSpec(memory_space=pltpu.HBM)
    working, across = pl.pallas_call(
        start_kernel,
        out_shape=(struct((2, HALF, COLS), bf16), struct((HALF, 128), bf16)),
        in_specs=[far] * 4,
        out_specs=(vmem, vmem),
        scratch_shapes=[
            pltpu.VMEM((2, HALF, COLS), bf16),
            pltpu.VMEM((2, HALF, COLS), f32),
            pltpu.VMEM((2, HALF, COLS), f32),
            pltpu.VMEM((RANK, COLS), bf16),
            pltpu.SemaphoreType.DMA((3 * START_STEPS + 1,)),
        ],
        compiler_params=params,
    )(*(pltpu.with_memory_space_constraint(x, pltpu.HBM) for x in (video, sparse, multiplier, start_block.T)))

    across = exchange(across, "frm")
    across = whole(functools.partial(sum_kernel, FRM), struct((HALF, 128), bf16), 1)(across)
    across = exchange(across, "frm")

    krylov = whole(krylov_kernel, struct((128, 128)), 2)(across, working)
    krylov = exchange(krylov, "pix")
    krylov = whole(functools.partial(sum_kernel, PIX), struct((128, 128)), 1)(krylov)
    krylov = exchange(krylov, "pix")

    wide = struct((FRM * CHUNK, 128))
    krylov, projected = whole(project_kernel, (struct((RANK, COLS)), wide), 2)(krylov, working)
    projected = exchange(projected, "frm")
    projected = whole(functools.partial(sum_kernel, FRM), wide, 1)(projected)
    projected = exchange(projected, "frm")

    projected, subspace, grams = whole(
        basis_kernel,
        (struct((HALF, 128)), struct((RANK, COLS)), struct((PIX * 32, 128), bf16)),
        2,
        scratch_shapes=[pltpu.VMEM((RANK, 128), f32)],
    )(projected, krylov)
    grams = exchange(grams, "pix")

    sparse_next, multiplier_next, sums = pl.pallas_call(
        finish_kernel,
        out_shape=(struct((2, HALF, COLS)), struct((2, HALF, COLS)), struct((PIX * 8, 128))),
        in_specs=[vmem] * 5,
        out_specs=(far, far, vmem),
        scratch_shapes=[pltpu.VMEM((2, 2, HALF, COLS), f32), pltpu.SemaphoreType.DMA((4 * STEPS,))],
        compiler_params=params,
    )(grams, subspace, video, multiplier, projected)
    sums = exchange(sums, "pix")
    ratio = whole(ratio_kernel, struct((2, 128)), 1)(sums)

    shape = (ROWS, COLS)
    return sparse_next.reshape(shape), multiplier_next.reshape(shape), ratio.reshape(COLS)


def solution(mesh):
    placed = (P("pix", "frm"), P("pix", "frm"), P("pix", "frm"), P("frm", None))
    return jax.shard_map(
        per_device,
        mesh=mesh,
        in_specs=placed,
        out_specs=(P("pix", "frm"), P("pix", "frm"), P("frm")),
        check_vma=False,
    )
```

```python
import functools

import jax
import jax.numpy as jnp
from jax import lax
from jax.experimental import pallas as pl
from jax.experimental.pallas import tpu as pltpu
from jax.sharding import PartitionSpec as P

mu_value = 1.25
inverse_mu = 0.8
sparse_cut = 0.8
shrink_ratio = 0.25
epsilon_value = 1e-06

f32 = jnp.float32
bf16 = jnp.bfloat16
highest = lax.Precision.HIGHEST

FRM = 32
PIX = 16
ROWS = 1024
HALF = 512
COLS = 256
RANK = 64
START_STEPS = 2
START_TILE = HALF // START_STEPS
STEPS = 4
TILE = HALF // STEPS
SLICE = HALF // FRM
CHUNK = SLICE + 1

vmem = pl.BlockSpec(memory_space=pltpu.VMEM)
params = pltpu.CompilerParams(vmem_limit_bytes=40 * 1024 * 1024)


def dot_nt(a, b, **kw):
    return lax.dot_general(a, b, (((1,), (1,)), ((), ())), preferred_element_type=f32, **kw)


def dot_tn(a, b, **kw):
    return lax.dot_general(a, b, (((0,), (0,)), ((), ())), preferred_element_type=f32, **kw)


def dot_nn(a, b, **kw):
    return lax.dot_general(a, b, (((1,), (0,)), ((), ())), preferred_element_type=f32, **kw)


def split_two(x):
    hi = x.astype(bf16)
    return hi, (x - hi.astype(f32)).astype(bf16)


def split_three(x):
    hi = x.astype(bf16)
    rest = x - hi.astype(f32)
    mid = rest.astype(bf16)
    return hi, mid, (rest - mid.astype(f32)).astype(bf16)


def sub_iota():
    return lax.broadcasted_iota(jnp.int32, (8, 128), 0)


def lane_iota():
    return lax.broadcasted_iota(jnp.int32, (8, 128), 1)


def row_of(x, k):
    return jnp.broadcast_to(x[k : k + 1, :], (8, 128))


def column_of(x, c):
    return jnp.broadcast_to(x[:, c : c + 1], (8, 128))


def augment(a):
    blocks = []
    for b in range(8):
        eye = jnp.where(lane_iota() == sub_iota() + (8 * b + 64), 1.0, 0.0).astype(f32)
        part = a[8 * b : 8 * b + 8]
        blocks.append(jnp.where(lane_iota() < 64, jnp.concatenate([part, part], axis=1), eye))
    return blocks


def fold(block, cols, rows):
    terms = [col * row for col, row in zip(cols, rows)]
    while len(terms) > 1:
        terms = [x + y for x, y in zip(terms[::2], terms[1::2])]
    return block - terms[0]


def rows_of(x):
    return [row_of(x, j) for j in range(8)]


def invert(blocks):
    blocks = list(blocks)
    sub = sub_iota()
    for b in range(8):
        lead = blocks[b]
        cols = [column_of(lead, 8 * b + j) for j in range(8)]
        others = [i % 8 for i in range(b + 1, b + 8)]
        mults = {i: [column_of(blocks[i], 8 * b + j) for j in range(8)] for i in others}
        for k in range(8):
            inverse = 1.0 / row_of(cols[k], k)
            mult = cols[k] * inverse
            for j in range(k + 1, 8):
                row = row_of(cols[j], k)
                cols[j] = jnp.where(sub == k, row * inverse, cols[j] - mult * row)
            row = row_of(lead, k)
            lead = jnp.where(sub == k, row * inverse, lead - mult * row)
        blocks[b] = lead
        lead_rows = rows_of(lead)
        for i in others:
            blocks[i] = fold(blocks[i], mults[i], lead_rows)
    return blocks


def factorize(blocks):
    blocks = [list(block) for block in blocks]
    sub = sub_iota()
    rows = []
    cols = [column_of(blocks[0][0], j) for j in range(8)]
    for b in range(8):
        lead, last = blocks[b], b == 7
        mults = {i: [column_of(blocks[i][0], 8 * b + j) for j in range(8)] for i in range(b + 1, 8)}
        if not last:
            ahead = [column_of(blocks[b + 1][0], 8 * b + 8 + j) for j in range(8)]
            cols = cols + [column_of(lead[0], 8 * b + 8 + j) for j in range(8)]
        for k in range(8):
            lead_row = [row_of(x, k) for x in lead]
            root = lax.rsqrt(row_of(cols[k], k))
            rows.append([x * root for x in lead_row])
            inverse = root * root
            mult = cols[k] * inverse
            for j in range(k + 1, len(cols)):
                row = row_of(cols[j], k)
                cols[j] = jnp.where(sub == k, row * inverse, cols[j] - mult * row)
            lead = [jnp.where(sub == k, y * inverse, x - mult * y) for x, y in zip(lead, lead_row)]
        if last:
            break
        cols = [fold(ahead[j], mults[b + 1], rows_of(cols[8 + j])) for j in range(8)]
        lead_rows = [rows_of(x) for x in lead]
        for i in range(b + 1, 8):
            blocks[i] = [fold(x, mults[i], y) for x, y in zip(blocks[i], lead_rows)]
    return rows


def start_kernel(video, sparse, multiplier, start, working, across, video_in, sparse_in, multiplier_in, start_in, sems):
    sources = ((video, video_in), (sparse, sparse_in), (multiplier, multiplier_in))
    copies = [pltpu.make_async_copy(start, start_in, sems.at[3 * START_STEPS])]
    for i in range(START_STEPS):
        rows = pl.ds(START_TILE * i, START_TILE)
        for j, (source, target) in enumerate(sources):
            copies.append(pltpu.make_async_copy(source.at[:, rows], target.at[:, rows], sems.at[3 * i + j]))
    for copy in copies:
        copy.start()
    copies[0].wait()
    for i in range(START_STEPS):
        rows = slice(START_TILE * i, START_TILE * i + START_TILE)
        for copy in copies[1 + 3 * i : 4 + 3 * i]:
            copy.wait()
        halves = []
        for h in range(2):
            value = video_in[h, rows].astype(f32) - sparse_in[h, rows] + multiplier_in[h, rows] * inverse_mu
            value = value.astype(bf16)
            working[h, rows] = value
            halves.append(dot_nt(value, start_in[...]))
        across[rows] = jnp.concatenate(halves, axis=1).astype(bf16)


def sum_kernel(peers, x, out):
    rows = x.shape[0] // peers
    total = x[:rows].astype(f32)
    for i in range(1, peers):
        total = total + x[rows * i : rows * i + rows].astype(f32)
    total = total.astype(out.dtype)
    for i in range(peers):
        out[rows * i : rows * i + rows] = total


def krylov_kernel(across, working, out):
    packed = across[...]
    first = dot_tn(packed, working[0])
    second = dot_tn(packed, working[1])
    krylov = first[:RANK] + second[RANK:]
    for i in range(8):
        out[8 * i : 8 * i + 8] = krylov[8 * i : 8 * i + 8, :128]
        out[RANK + 8 * i : RANK + 8 * i + 8] = krylov[8 * i : 8 * i + 8, 128:]


def project_kernel(gathered, working, krylov_out, out):
    packed = gathered[...]
    krylov = jnp.concatenate([packed[:RANK], packed[RANK:]], axis=1)
    krylov_out[...] = krylov
    zero = jnp.zeros((RANK, COLS), bf16)
    first, second, third = split_three(krylov)
    low = dot_nt(working[0], jnp.concatenate([first, zero, second, zero], axis=0))
    high = dot_nt(working[1], jnp.concatenate([zero, first, zero, second], axis=0))
    total = dot_nt(working[0], jnp.concatenate([third, zero], axis=0))
    total = total + dot_nt(working[1], jnp.concatenate([zero, third], axis=0))
    total = (total + (low[:, 128:] + high[:, 128:])) + (low[:, :128] + high[:, :128])
    gram = dot_nt(krylov, krylov, precision=highest)
    gram = jnp.concatenate([gram[:32], gram[32:]], axis=1)
    for i in range(FRM):
        at = CHUNK * i
        out[at : at + SLICE] = total[SLICE * i : SLICE * i + SLICE]
        out[at + SLICE : at + CHUNK] = gram[i : i + 1]


def basis_kernel(gathered, krylov, projected_out, subspace_out, out, rows_ref):
    gram = jnp.concatenate([gathered[CHUNK * i + SLICE : CHUNK * i + CHUNK] for i in range(FRM)], axis=0)
    gram = jnp.concatenate([gram[:, :RANK], gram[:, RANK:]], axis=0)
    for i, row in enumerate(factorize([[block] for block in augment(gram)])):
        rows_ref[i : i + 1] = row[0][0:1]
    inverse = rows_ref[:, RANK:]
    zero = jnp.zeros((RANK, RANK), f32)
    pair = jnp.concatenate(
        [jnp.concatenate([inverse, zero], axis=1), jnp.concatenate([zero, inverse], axis=1)], axis=0
    )
    packed = jnp.concatenate([gathered[CHUNK * i : CHUNK * i + SLICE] for i in range(FRM)], axis=0)
    left = split_three(packed)
    right = split_three(pair)
    outer = jnp.concatenate(right[:2], axis=0)
    projected = dot_nt(jnp.concatenate(left[:2], axis=1), jnp.concatenate([outer, outer], axis=1))
    rest = dot_nt(jnp.concatenate([left[0], left[2]], axis=1), jnp.concatenate([right[2], right[0]], axis=1))
    projected = projected[:, :128] + (projected[:, 128:] + rest)
    projected_out[...] = projected
    subspace_out[...] = dot_nn(inverse, krylov[...], precision=highest)
    hi, lo = split_two(projected)
    gram = dot_tn(hi, hi) + (dot_tn(hi, lo) + dot_tn(lo, hi))
    gram = gram[:RANK, :RANK] + gram[RANK:, RANK:]
    gram = jnp.concatenate([gram[:32], gram[32:]], axis=1).astype(bf16)
    for i in range(PIX):
        out[32 * i : 32 * i + 32] = gram


def finish_kernel(grams, subspace, video, multiplier, projected, sparse_out, multiplier_out, out, near, rows_ref, sems):
    gram = grams[:32].astype(f32)
    for i in range(1, PIX):
        gram = gram + grams[32 * i : 32 * i + 32].astype(f32)
    gram = jnp.concatenate([gram[:, :RANK], gram[:, RANK:]], axis=0)
    rows = lax.broadcasted_iota(jnp.int32, (RANK, RANK), 0)
    cols = lax.broadcasted_iota(jnp.int32, (RANK, RANK), 1)
    eye = jnp.where(rows == cols, 1.0, 0.0).astype(f32)
    level = jnp.sum(jnp.sum(gram * eye, axis=0, keepdims=True), axis=1, keepdims=True) * (shrink_ratio / RANK)
    wide = [subspace[8 * i : 8 * i + 8] for i in range(8)]
    blocks = [[x, y[:, :128], y[:, 128:]] for x, y in zip(augment(gram + level * eye), wide)]
    for i, row in enumerate(factorize(blocks)):
        for j in range(3):
            rows_ref[i : i + 1, 128 * j : 128 * j + 128] = row[j][0:1]
    mixed = subspace[...] - level * dot_tn(rows_ref[:, RANK:128], rows_ref[:, 128:], precision=highest)
    zero = jnp.zeros((RANK, COLS), bf16)
    parts = split_two(mixed)
    weighted = [[jnp.concatenate(pair, axis=0) for pair in ((part, zero), (zero, part))] for part in parts]
    weighted[0] = [jnp.concatenate([pair, pair], axis=0) for pair in weighted[0]]

    residual_sq = jnp.zeros((8, COLS), f32)
    video_sq = jnp.zeros((8, COLS), f32)
    copies = []
    for i in range(STEPS):
        rows = slice(TILE * i, TILE * i + TILE)
        hi, lo = split_two(projected[rows])
        both = jnp.concatenate([hi, lo], axis=1)
        for h in range(2):
            low_rank = dot_nn(both, weighted[0][h]) + dot_nn(hi, weighted[1][h])
            video_full = video[h, rows].astype(f32)
            held = multiplier[h, rows]
            base = video_full - low_rank
            shifted = base + held * inverse_mu
            sparse_next = shifted - jnp.clip(shifted, -sparse_cut, sparse_cut)
            residual = base - sparse_next
            near[0, h, rows] = sparse_next
            near[1, h, rows] = held + mu_value * residual
            for j, target in enumerate((sparse_out, multiplier_out)):
                at = (h, pl.ds(TILE * i, TILE))
                copies.append(pltpu.make_async_copy(near.at[j].at[at], target.at[at], sems.at[len(copies)]))
                copies[-1].start()
            residual_sq += jnp.sum((residual * residual).reshape(TILE // 8, 8, COLS), axis=0)
            video_sq += jnp.sum((video_full * video_full).reshape(TILE // 8, 8, COLS), axis=0)
    residual_sq = jnp.sum(residual_sq, axis=0, keepdims=True)
    video_sq = jnp.sum(video_sq, axis=0, keepdims=True)
    tile = jnp.concatenate(
        [residual_sq[:, :128], residual_sq[:, 128:], video_sq[:, :128], video_sq[:, 128:], jnp.zeros((4, 128), f32)],
        axis=0,
    )
    for i in range(PIX):
        out[8 * i : 8 * i + 8] = tile
    for copy in copies:
        copy.wait()


def ratio_kernel(x, out):
    total = x[:8]
    for i in range(1, PIX):
        total = total + x[8 * i : 8 * i + 8]
    out[...] = jnp.sqrt(total[0:2] / (total[2:4] + epsilon_value))


def struct(shape, dtype=f32):
    return jax.ShapeDtypeStruct(shape, dtype)


def whole(kernel, outs, count, **kw):
    return pl.pallas_call(
        kernel,
        out_shape=outs,
        in_specs=[vmem] * count,
        out_specs=jax.tree.map(lambda _: vmem, outs),
        compiler_params=params,
        **kw,
    )


def exchange(x, axis):
    peers = FRM if axis == "frm" else PIX
    parts = (peers, 1, -1) if x.dtype == f32 else (peers, -1, 128)
    return lax.all_to_all(x.reshape(parts), axis, 0, 0).reshape(x.shape)


def per_device(video, sparse, multiplier, start_block):
    video, sparse, multiplier = (x.reshape(2, HALF, COLS) for x in (video, sparse, multiplier))
    far = pl.BlockSpec(memory_space=pltpu.HBM)
    working, across = pl.pallas_call(
        start_kernel,
        out_shape=(struct((2, HALF, COLS), bf16), struct((HALF, 128), bf16)),
        in_specs=[far] * 4,
        out_specs=(vmem, vmem),
        scratch_shapes=[
            pltpu.VMEM((2, HALF, COLS), bf16),
            pltpu.VMEM((2, HALF, COLS), f32),
            pltpu.VMEM((2, HALF, COLS), f32),
            pltpu.VMEM((RANK, COLS), bf16),
            pltpu.SemaphoreType.DMA((3 * START_STEPS + 1,)),
        ],
        compiler_params=params,
    )(*(pltpu.with_memory_space_constraint(x, pltpu.HBM) for x in (video, sparse, multiplier, start_block.T)))

    across = exchange(across, "frm")
    across = whole(functools.partial(sum_kernel, FRM), struct((HALF, 128), bf16), 1)(across)
    across = exchange(across, "frm")

    krylov = whole(krylov_kernel, struct((128, 128)), 2)(across, working)
    krylov = exchange(krylov, "pix")
    krylov = whole(functools.partial(sum_kernel, PIX), struct((128, 128)), 1)(krylov)
    krylov = exchange(krylov, "pix")

    wide = struct((FRM * CHUNK, 128))
    krylov, projected = whole(project_kernel, (struct((RANK, COLS)), wide), 2)(krylov, working)
    projected = exchange(projected, "frm")
    projected = whole(functools.partial(sum_kernel, FRM), wide, 1)(projected)
    projected = exchange(projected, "frm")

    projected, subspace, grams = whole(
        basis_kernel,
        (struct((HALF, 128)), struct((RANK, COLS)), struct((PIX * 32, 128), bf16)),
        2,
        scratch_shapes=[pltpu.VMEM((RANK, 128), f32)],
    )(projected, krylov)
    grams = exchange(grams, "pix")

    sparse_next, multiplier_next, sums = pl.pallas_call(
        finish_kernel,
        out_shape=(struct((2, HALF, COLS)), struct((2, HALF, COLS)), struct((PIX * 8, 128))),
        in_specs=[vmem] * 5,
        out_specs=(far, far, vmem),
        scratch_shapes=[pltpu.VMEM((2, 2, HALF, COLS), f32), pltpu.VMEM((RANK, 3 * 128), f32), pltpu.SemaphoreType.DMA((4 * STEPS,))],
        compiler_params=params,
    )(grams, subspace, video, multiplier, projected)
    sums = exchange(sums, "pix")
    ratio = whole(ratio_kernel, struct((2, 128)), 1)(sums)

    shape = (ROWS, COLS)
    return sparse_next.reshape(shape), multiplier_next.reshape(shape), ratio.reshape(COLS)


def solution(mesh):
    placed = (P("pix", "frm"), P("pix", "frm"), P("pix", "frm"), P("frm", None))
    return jax.shard_map(
        per_device,
        mesh=mesh,
        in_specs=placed,
        out_specs=(P("pix", "frm"), P("pix", "frm"), P("frm")),
        check_vma=False,
    )
```

```python
import functools

import jax
import jax.numpy as jnp
from jax import lax
from jax.experimental import pallas as pl
from jax.experimental.pallas import tpu as pltpu
from jax.sharding import PartitionSpec as P

mu_value = 1.25
inverse_mu = 0.8
sparse_cut = 0.8
shrink_ratio = 0.25
epsilon_value = 1e-06

f32 = jnp.float32
bf16 = jnp.bfloat16
highest = lax.Precision.HIGHEST

FRM = 32
PIX = 16
ROWS = 1024
HALF = 512
COLS = 256
RANK = 64
START_STEPS = 2
START_TILE = HALF // START_STEPS
STEPS = 4
TILE = HALF // STEPS
SLICE = HALF // FRM
CHUNK = SLICE + 1

vmem = pl.BlockSpec(memory_space=pltpu.VMEM)
params = pltpu.CompilerParams(vmem_limit_bytes=40 * 1024 * 1024)


def dot_nt(a, b, **kw):
    return lax.dot_general(a, b, (((1,), (1,)), ((), ())), preferred_element_type=f32, **kw)


def dot_tn(a, b, **kw):
    return lax.dot_general(a, b, (((0,), (0,)), ((), ())), preferred_element_type=f32, **kw)


def dot_nn(a, b, **kw):
    return lax.dot_general(a, b, (((1,), (0,)), ((), ())), preferred_element_type=f32, **kw)


def split_two(x):
    hi = x.astype(bf16)
    return hi, (x - hi.astype(f32)).astype(bf16)


def split_three(x):
    hi = x.astype(bf16)
    rest = x - hi.astype(f32)
    mid = rest.astype(bf16)
    return hi, mid, (rest - mid.astype(f32)).astype(bf16)


def sub_iota():
    return lax.broadcasted_iota(jnp.int32, (8, 128), 0)


def lane_iota():
    return lax.broadcasted_iota(jnp.int32, (8, 128), 1)


def row_of(x, k):
    return jnp.broadcast_to(x[k : k + 1, :], (8, 128))


def column_of(x, c):
    return jnp.broadcast_to(x[:, c : c + 1], (8, 128))


def augment(a):
    blocks = []
    for b in range(8):
        eye = jnp.where(lane_iota() == sub_iota() + (8 * b + 64), 1.0, 0.0).astype(f32)
        part = a[8 * b : 8 * b + 8]
        blocks.append(jnp.where(lane_iota() < 64, jnp.concatenate([part, part], axis=1), eye))
    return blocks


def fold(block, cols, rows):
    terms = [col * row for col, row in zip(cols, rows)]
    while len(terms) > 1:
        terms = [x + y for x, y in zip(terms[::2], terms[1::2])]
    return block - terms[0]


def rows_of(x):
    return [row_of(x, j) for j in range(8)]


def invert(blocks):
    blocks = list(blocks)
    sub = sub_iota()
    for b in range(8):
        lead = blocks[b]
        cols = [column_of(lead, 8 * b + j) for j in range(8)]
        others = [i % 8 for i in range(b + 1, b + 8)]
        mults = {i: [column_of(blocks[i], 8 * b + j) for j in range(8)] for i in others}
        for k in range(8):
            inverse = 1.0 / row_of(cols[k], k)
            mult = cols[k] * inverse
            for j in range(k + 1, 8):
                row = row_of(cols[j], k)
                cols[j] = jnp.where(sub == k, row * inverse, cols[j] - mult * row)
            row = row_of(lead, k)
            lead = jnp.where(sub == k, row * inverse, lead - mult * row)
        blocks[b] = lead
        lead_rows = rows_of(lead)
        for i in others:
            blocks[i] = fold(blocks[i], mults[i], lead_rows)
    return blocks


def factorize(blocks):
    blocks = [list(block) for block in blocks]
    sub = sub_iota()
    rows = []
    cols = [column_of(blocks[0][0], j) for j in range(8)]
    for b in range(8):
        lead, last = blocks[b], b == 7
        mults = {i: [column_of(blocks[i][0], 8 * b + j) for j in range(8)] for i in range(b + 1, 8)}
        if not last:
            ahead = [column_of(blocks[b + 1][0], 8 * b + 8 + j) for j in range(8)]
            cols = cols + [column_of(lead[0], 8 * b + 8 + j) for j in range(8)]
        for k in range(8):
            lead_row = [row_of(x, k) for x in lead]
            root = lax.rsqrt(row_of(cols[k], k))
            rows.append([x * root for x in lead_row])
            inverse = root * root
            mult = cols[k] * inverse
            for j in range(k + 1, len(cols)):
                row = row_of(cols[j], k)
                cols[j] = jnp.where(sub == k, row * inverse, cols[j] - mult * row)
            lead = [jnp.where(sub == k, y * inverse, x - mult * y) for x, y in zip(lead, lead_row)]
        if last:
            break
        cols = [fold(ahead[j], mults[b + 1], rows_of(cols[8 + j])) for j in range(8)]
        lead_rows = [rows_of(x) for x in lead]
        for i in range(b + 1, 8):
            blocks[i] = [fold(x, mults[i], y) for x, y in zip(blocks[i], lead_rows)]
    return rows


def start_kernel(video, sparse, multiplier, start, working, across, video_in, sparse_in, multiplier_in, start_in, sems):
    sources = ((video, video_in), (sparse, sparse_in), (multiplier, multiplier_in))
    copies = [pltpu.make_async_copy(start, start_in, sems.at[3 * START_STEPS])]
    for i in range(START_STEPS):
        rows = pl.ds(START_TILE * i, START_TILE)
        for j, (source, target) in enumerate(sources):
            copies.append(pltpu.make_async_copy(source.at[:, rows], target.at[:, rows], sems.at[3 * i + j]))
    for copy in copies:
        copy.start()
    copies[0].wait()
    for i in range(START_STEPS):
        rows = slice(START_TILE * i, START_TILE * i + START_TILE)
        for copy in copies[1 + 3 * i : 4 + 3 * i]:
            copy.wait()
        halves = []
        for h in range(2):
            value = video_in[h, rows].astype(f32) - sparse_in[h, rows] + multiplier_in[h, rows] * inverse_mu
            value = value.astype(bf16)
            working[h, rows] = value
            halves.append(dot_nt(value, start_in[...]))
        across[rows] = jnp.concatenate(halves, axis=1).astype(bf16)


def sum_kernel(peers, x, out):
    rows = x.shape[0] // peers
    total = x[:rows].astype(f32)
    for i in range(1, peers):
        total = total + x[rows * i : rows * i + rows].astype(f32)
    total = total.astype(out.dtype)
    for i in range(peers):
        out[rows * i : rows * i + rows] = total


def krylov_kernel(across, working, out):
    packed = across[...]
    first = dot_tn(packed, working[0])
    second = dot_tn(packed, working[1])
    krylov = first[:RANK] + second[RANK:]
    for i in range(8):
        out[8 * i : 8 * i + 8] = krylov[8 * i : 8 * i + 8, :128]
        out[RANK + 8 * i : RANK + 8 * i + 8] = krylov[8 * i : 8 * i + 8, 128:]


def project_kernel(gathered, working, krylov_out, out):
    packed = gathered[...]
    krylov = jnp.concatenate([packed[:RANK], packed[RANK:]], axis=1)
    krylov_out[...] = krylov
    zero = jnp.zeros((RANK, COLS), bf16)
    first, second, third = split_three(krylov)
    low = dot_nt(working[0], jnp.concatenate([first, zero, second, zero], axis=0))
    high = dot_nt(working[1], jnp.concatenate([zero, first, zero, second], axis=0))
    total = dot_nt(working[0], jnp.concatenate([third, zero], axis=0))
    total = total + dot_nt(working[1], jnp.concatenate([zero, third], axis=0))
    total = (total + (low[:, 128:] + high[:, 128:])) + (low[:, :128] + high[:, :128])
    gram = dot_nt(krylov, krylov, precision=highest)
    gram = jnp.concatenate([gram[:32], gram[32:]], axis=1)
    for i in range(FRM):
        at = CHUNK * i
        out[at : at + SLICE] = total[SLICE * i : SLICE * i + SLICE]
        out[at + SLICE : at + CHUNK] = gram[i : i + 1]


def basis_kernel(gathered, krylov, projected_out, subspace_out, out, rows_ref):
    gram = jnp.concatenate([gathered[CHUNK * i + SLICE : CHUNK * i + CHUNK] for i in range(FRM)], axis=0)
    gram = jnp.concatenate([gram[:, :RANK], gram[:, RANK:]], axis=0)
    for i, row in enumerate(factorize([[block] for block in augment(gram)])):
        rows_ref[i : i + 1] = row[0][0:1]
    inverse = rows_ref[:, RANK:]
    zero = jnp.zeros((RANK, RANK), f32)
    pair = jnp.concatenate(
        [jnp.concatenate([inverse, zero], axis=1), jnp.concatenate([zero, inverse], axis=1)], axis=0
    )
    packed = jnp.concatenate([gathered[CHUNK * i : CHUNK * i + SLICE] for i in range(FRM)], axis=0)
    left = split_three(packed)
    right = split_three(pair)
    outer = jnp.concatenate(right[:2], axis=0)
    projected = dot_nt(jnp.concatenate(left[:2], axis=1), jnp.concatenate([outer, outer], axis=1))
    rest = dot_nt(jnp.concatenate([left[0], left[2]], axis=1), jnp.concatenate([right[2], right[0]], axis=1))
    projected = projected[:, :128] + (projected[:, 128:] + rest)
    projected_out[...] = projected
    subspace_out[...] = dot_nn(inverse, krylov[...], precision=highest)
    hi, lo = split_two(projected)
    gram = dot_tn(hi, hi) + (dot_tn(hi, lo) + dot_tn(lo, hi))
    gram = gram[:RANK, :RANK] + gram[RANK:, RANK:]
    gram = jnp.concatenate([gram[:32], gram[32:]], axis=1).astype(bf16)
    for i in range(PIX):
        out[32 * i : 32 * i + 32] = gram


def finish_kernel(grams, subspace, video, multiplier, projected, sparse_out, multiplier_out, out, near, rows_ref, sems):
    gram = grams[:32].astype(f32)
    for i in range(1, PIX):
        gram = gram + grams[32 * i : 32 * i + 32].astype(f32)
    gram = jnp.concatenate([gram[:, :RANK], gram[:, RANK:]], axis=0)
    rows = lax.broadcasted_iota(jnp.int32, (RANK, RANK), 0)
    cols = lax.broadcasted_iota(jnp.int32, (RANK, RANK), 1)
    eye = jnp.where(rows == cols, 1.0, 0.0).astype(f32)
    level = jnp.sum(jnp.sum(gram * eye, axis=0, keepdims=True), axis=1, keepdims=True) * (shrink_ratio / RANK)
    wide = [subspace[8 * i : 8 * i + 8] for i in range(8)]
    blocks = [[x, y[:, :128], y[:, 128:]] for x, y in zip(augment(gram + level * eye), wide)]
    for i, row in enumerate(factorize(blocks)):
        for j in range(3):
            rows_ref[i : i + 1, 128 * j : 128 * j + 128] = row[j][0:1]
    mixed = subspace[...] - level * dot_tn(rows_ref[:, RANK:128], rows_ref[:, 128:], precision=highest)
    zero = jnp.zeros((RANK, COLS), bf16)
    parts = split_two(mixed)
    weighted = [[jnp.concatenate(pair, axis=0) for pair in ((part, zero), (zero, part))] for part in parts]
    weighted[0] = [jnp.concatenate([pair, pair], axis=0) for pair in weighted[0]]

    residual_sq = jnp.zeros((8, COLS), f32)
    video_sq = jnp.zeros((8, COLS), f32)
    copies = []
    for i in range(STEPS):
        rows = slice(TILE * i, TILE * i + TILE)
        hi, lo = split_two(projected[rows])
        both = jnp.concatenate([hi, lo], axis=1)
        for h in range(2):
            low_rank = dot_nn(both, weighted[0][h]) + dot_nn(hi, weighted[1][h])
            video_full = video[h, rows].astype(f32)
            held = multiplier[h, rows]
            base = video_full - low_rank
            shifted = base + held * inverse_mu
            sparse_next = shifted - jnp.clip(shifted, -sparse_cut, sparse_cut)
            residual = base - sparse_next
            near[0, h, rows] = sparse_next
            near[1, h, rows] = held + mu_value * residual
            for j, target in enumerate((sparse_out, multiplier_out)):
                at = (h, pl.ds(TILE * i, TILE))
                copies.append(pltpu.make_async_copy(near.at[j].at[at], target.at[at], sems.at[len(copies)]))
                copies[-1].start()
            residual_sq += jnp.sum((residual * residual).reshape(TILE // 8, 8, COLS), axis=0)
            video_sq += jnp.sum((video_full * video_full).reshape(TILE // 8, 8, COLS), axis=0)
    residual_sq = jnp.sum(residual_sq, axis=0, keepdims=True)
    video_sq = jnp.sum(video_sq, axis=0, keepdims=True)
    tile = jnp.concatenate(
        [residual_sq[:, :128], residual_sq[:, 128:], video_sq[:, :128], video_sq[:, 128:]],
        axis=0,
    )
    for i in range(PIX):
        out[4 * i : 4 * i + 4] = tile
    for copy in copies:
        copy.wait()


def ratio_kernel(x, out):
    total = x[:4]
    for i in range(1, PIX):
        total = total + x[4 * i : 4 * i + 4]
    out[...] = jnp.sqrt(total[0:2] / (total[2:4] + epsilon_value))


def struct(shape, dtype=f32):
    return jax.ShapeDtypeStruct(shape, dtype)


def whole(kernel, outs, count, **kw):
    return pl.pallas_call(
        kernel,
        out_shape=outs,
        in_specs=[vmem] * count,
        out_specs=jax.tree.map(lambda _: vmem, outs),
        compiler_params=params,
        **kw,
    )


def exchange(x, axis):
    peers = FRM if axis == "frm" else PIX
    parts = (peers, 1, -1) if x.dtype == f32 else (peers, -1, 128)
    index = [[p * FRM + f for f in range(FRM)] for p in range(PIX)]
    groups = index if axis == "frm" else [list(group) for group in zip(*index)]
    return lax.all_to_all(x.reshape(parts), ("pix", "frm"), 0, 0, axis_index_groups=groups).reshape(x.shape)


def per_device(video, sparse, multiplier, start_block):
    video, sparse, multiplier = (x.reshape(2, HALF, COLS) for x in (video, sparse, multiplier))
    far = pl.BlockSpec(memory_space=pltpu.HBM)
    working, across = pl.pallas_call(
        start_kernel,
        out_shape=(struct((2, HALF, COLS), bf16), struct((HALF, 128), bf16)),
        in_specs=[far] * 4,
        out_specs=(vmem, vmem),
        scratch_shapes=[
            pltpu.VMEM((2, HALF, COLS), bf16),
            pltpu.VMEM((2, HALF, COLS), f32),
            pltpu.VMEM((2, HALF, COLS), f32),
            pltpu.VMEM((RANK, COLS), bf16),
            pltpu.SemaphoreType.DMA((3 * START_STEPS + 1,)),
        ],
        compiler_params=params,
    )(*(pltpu.with_memory_space_constraint(x, pltpu.HBM) for x in (video, sparse, multiplier, start_block.T)))

    across = exchange(across, "frm")
    across = whole(functools.partial(sum_kernel, FRM), struct((HALF, 128), bf16), 1)(across)
    across = exchange(across, "frm")

    krylov = whole(krylov_kernel, struct((128, 128)), 2)(across, working)
    krylov = exchange(krylov, "pix")
    krylov = whole(functools.partial(sum_kernel, PIX), struct((128, 128)), 1)(krylov)
    krylov = exchange(krylov, "pix")

    wide = struct((FRM * CHUNK, 128))
    krylov, projected = whole(project_kernel, (struct((RANK, COLS)), wide), 2)(krylov, working)
    projected = exchange(projected, "frm")
    projected = whole(functools.partial(sum_kernel, FRM), wide, 1)(projected)
    projected = exchange(projected, "frm")

    projected, subspace, grams = whole(
        basis_kernel,
        (struct((HALF, 128)), struct((RANK, COLS)), struct((PIX * 32, 128), bf16)),
        2,
        scratch_shapes=[pltpu.VMEM((RANK, 128), f32)],
    )(projected, krylov)
    grams = exchange(grams, "pix")

    sparse_next, multiplier_next, sums = pl.pallas_call(
        finish_kernel,
        out_shape=(struct((2, HALF, COLS)), struct((2, HALF, COLS)), struct((PIX * 4, 128))),
        in_specs=[vmem] * 5,
        out_specs=(far, far, vmem),
        scratch_shapes=[pltpu.VMEM((2, 2, HALF, COLS), f32), pltpu.VMEM((RANK, 3 * 128), f32), pltpu.SemaphoreType.DMA((4 * STEPS,))],
        compiler_params=params,
    )(grams, subspace, video, multiplier, projected)
    sums = exchange(sums, "pix")
    ratio = whole(ratio_kernel, struct((2, 128)), 1)(sums)

    shape = (ROWS, COLS)
    return sparse_next.reshape(shape), multiplier_next.reshape(shape), ratio.reshape(COLS)


def solution(mesh):
    placed = (P("pix", "frm"), P("pix", "frm"), P("pix", "frm"), P("frm", None))
    return jax.shard_map(
        per_device,
        mesh=mesh,
        in_specs=placed,
        out_specs=(P("pix", "frm"), P("pix", "frm"), P("frm")),
        check_vma=False,
    )
```

```python
import functools

import jax
import jax.numpy as jnp
from jax import lax
from jax.experimental import pallas as pl
from jax.experimental.pallas import tpu as pltpu
from jax.sharding import PartitionSpec as P

mu_value = 1.25
inverse_mu = 0.8
sparse_cut = 0.8
shrink_ratio = 0.25
epsilon_value = 1e-06

f32 = jnp.float32
bf16 = jnp.bfloat16
highest = lax.Precision.HIGHEST

FRM = 32
PIX = 16
ROWS = 1024
HALF = 512
COLS = 256
RANK = 64
START_STEPS = 2
START_TILE = HALF // START_STEPS
STEPS = 4
TILE = HALF // STEPS
SLICE = HALF // FRM
CHUNK = SLICE + 1

vmem = pl.BlockSpec(memory_space=pltpu.VMEM)
params = pltpu.CompilerParams(vmem_limit_bytes=40 * 1024 * 1024)


def dot_nt(a, b, **kw):
    return lax.dot_general(a, b, (((1,), (1,)), ((), ())), preferred_element_type=f32, **kw)


def dot_tn(a, b, **kw):
    return lax.dot_general(a, b, (((0,), (0,)), ((), ())), preferred_element_type=f32, **kw)


def dot_nn(a, b, **kw):
    return lax.dot_general(a, b, (((1,), (0,)), ((), ())), preferred_element_type=f32, **kw)


def split_two(x):
    hi = x.astype(bf16)
    return hi, (x - hi.astype(f32)).astype(bf16)


def split_three(x):
    hi = x.astype(bf16)
    rest = x - hi.astype(f32)
    mid = rest.astype(bf16)
    return hi, mid, (rest - mid.astype(f32)).astype(bf16)


def sub_iota():
    return lax.broadcasted_iota(jnp.int32, (8, 128), 0)


def lane_iota():
    return lax.broadcasted_iota(jnp.int32, (8, 128), 1)


def row_of(x, k):
    return jnp.broadcast_to(x[k : k + 1, :], (8, 128))


def column_of(x, c):
    return jnp.broadcast_to(x[:, c : c + 1], (8, 128))


def augment(a):
    blocks = []
    for b in range(8):
        eye = jnp.where(lane_iota() == sub_iota() + (8 * b + 64), 1.0, 0.0).astype(f32)
        part = a[8 * b : 8 * b + 8]
        blocks.append(jnp.where(lane_iota() < 64, jnp.concatenate([part, part], axis=1), eye))
    return blocks


def fold(block, cols, rows):
    terms = [col * row for col, row in zip(cols, rows)]
    while len(terms) > 1:
        terms = [x + y for x, y in zip(terms[::2], terms[1::2])]
    return block - terms[0]


def rows_of(x):
    return [row_of(x, j) for j in range(8)]


def invert(blocks):
    blocks = list(blocks)
    sub = sub_iota()
    for b in range(8):
        lead = blocks[b]
        cols = [column_of(lead, 8 * b + j) for j in range(8)]
        others = [i % 8 for i in range(b + 1, b + 8)]
        mults = {i: [column_of(blocks[i], 8 * b + j) for j in range(8)] for i in others}
        for k in range(8):
            inverse = 1.0 / row_of(cols[k], k)
            mult = cols[k] * inverse
            for j in range(k + 1, 8):
                row = row_of(cols[j], k)
                cols[j] = jnp.where(sub == k, row * inverse, cols[j] - mult * row)
            row = row_of(lead, k)
            lead = jnp.where(sub == k, row * inverse, lead - mult * row)
        blocks[b] = lead
        lead_rows = rows_of(lead)
        for i in others:
            blocks[i] = fold(blocks[i], mults[i], lead_rows)
    return blocks


def factorize(blocks):
    blocks = [list(block) for block in blocks]
    sub = sub_iota()
    rows = []
    cols = [column_of(blocks[0][0], j) for j in range(8)]
    for b in range(8):
        lead, last = blocks[b], b == 7
        mults = {i: [column_of(blocks[i][0], 8 * b + j) for j in range(8)] for i in range(b + 1, 8)}
        if not last:
            ahead = [column_of(blocks[b + 1][0], 8 * b + 8 + j) for j in range(8)]
            cols = cols + [column_of(lead[0], 8 * b + 8 + j) for j in range(8)]
        for k in range(8):
            lead_row = [row_of(x, k) for x in lead]
            root = lax.rsqrt(row_of(cols[k], k))
            rows.append([x * root for x in lead_row])
            inverse = root * root
            mult = cols[k] * inverse
            for j in range(k + 1, len(cols)):
                row = row_of(cols[j], k)
                cols[j] = jnp.where(sub == k, row * inverse, cols[j] - mult * row)
            lead = [jnp.where(sub == k, y * inverse, x - mult * y) for x, y in zip(lead, lead_row)]
        if last:
            break
        cols = [fold(ahead[j], mults[b + 1], rows_of(cols[8 + j])) for j in range(8)]
        lead_rows = [rows_of(x) for x in lead]
        for i in range(b + 1, 8):
            blocks[i] = [fold(x, mults[i], y) for x, y in zip(blocks[i], lead_rows)]
    return rows


def pack_symmetric(gram):
    wide = jnp.concatenate([gram[:32], gram[32:]], axis=1)
    free = (lane_iota() >= 64) & (lane_iota() < 96)
    tail = wide[24:]
    return jnp.concatenate(
        [jnp.where(free, pltpu.roll(tail, shift, 1), wide[8 * i : 8 * i + 8]) for i, shift in enumerate((64, 32, 96))],
        axis=0,
    )


def unpack_symmetric(packed):
    lane = lane_iota()
    first, second, third = (pltpu.roll(packed[8 * i : 8 * i + 8], shift, 1) for i, shift in enumerate((64, 96, 32)))
    tail = jnp.where(lane < 32, first, jnp.where(lane < 64, second, third))
    wide = jnp.concatenate([packed, tail], axis=0)
    upper = wide[:, :64]
    lower = jnp.concatenate([upper[:, 32:].T, wide[:, 96:]], axis=1)
    return jnp.concatenate([upper, lower], axis=0)


def start_kernel(video, sparse, multiplier, start, working, across, video_in, sparse_in, multiplier_in, start_in, sems):
    sources = ((video, video_in), (sparse, sparse_in), (multiplier, multiplier_in))
    copies = [pltpu.make_async_copy(start, start_in, sems.at[3 * START_STEPS])]
    for i in range(START_STEPS):
        rows = pl.ds(START_TILE * i, START_TILE)
        for j, (source, target) in enumerate(sources):
            copies.append(pltpu.make_async_copy(source.at[:, rows], target.at[:, rows], sems.at[3 * i + j]))
    for copy in copies:
        copy.start()
    copies[0].wait()
    for i in range(START_STEPS):
        rows = slice(START_TILE * i, START_TILE * i + START_TILE)
        for copy in copies[1 + 3 * i : 4 + 3 * i]:
            copy.wait()
        halves = []
        for h in range(2):
            value = video_in[h, rows].astype(f32) - sparse_in[h, rows] + multiplier_in[h, rows] * inverse_mu
            value = value.astype(bf16)
            working[h, rows] = value
            halves.append(dot_nt(value, start_in[...]))
        across[rows] = jnp.concatenate(halves, axis=1).astype(bf16)


def sum_kernel(peers, x, out):
    rows = x.shape[0] // peers
    total = x[:rows].astype(f32)
    for i in range(1, peers):
        total = total + x[rows * i : rows * i + rows].astype(f32)
    total = total.astype(out.dtype)
    for i in range(peers):
        out[rows * i : rows * i + rows] = total


def krylov_kernel(across, working, out):
    packed = across[...]
    first = dot_tn(packed, working[0])
    second = dot_tn(packed, working[1])
    krylov = first[:RANK] + second[RANK:]
    for i in range(8):
        out[8 * i : 8 * i + 8] = krylov[8 * i : 8 * i + 8, :128]
        out[RANK + 8 * i : RANK + 8 * i + 8] = krylov[8 * i : 8 * i + 8, 128:]


def project_kernel(gathered, working, krylov_out, out):
    packed = gathered[...]
    krylov = jnp.concatenate([packed[:RANK], packed[RANK:]], axis=1)
    krylov_out[...] = krylov
    zero = jnp.zeros((RANK, COLS), bf16)
    first, second, third = split_three(krylov)
    low = dot_nt(working[0], jnp.concatenate([first, zero, second, zero], axis=0))
    high = dot_nt(working[1], jnp.concatenate([zero, first, zero, second], axis=0))
    total = dot_nt(working[0], jnp.concatenate([third, zero], axis=0))
    total = total + dot_nt(working[1], jnp.concatenate([zero, third], axis=0))
    total = (total + (low[:, 128:] + high[:, 128:])) + (low[:, :128] + high[:, :128])
    gram = dot_nt(krylov, krylov, precision=highest)
    gram = jnp.concatenate([gram[:32], gram[32:]], axis=1)
    for i in range(FRM):
        at = CHUNK * i
        out[at : at + SLICE] = total[SLICE * i : SLICE * i + SLICE]
        out[at + SLICE : at + CHUNK] = gram[i : i + 1]


def basis_kernel(gathered, krylov, projected_out, subspace_out, out, rows_ref):
    gram = jnp.concatenate([gathered[CHUNK * i + SLICE : CHUNK * i + CHUNK] for i in range(FRM)], axis=0)
    gram = jnp.concatenate([gram[:, :RANK], gram[:, RANK:]], axis=0)
    for i, row in enumerate(factorize([[block] for block in augment(gram)])):
        rows_ref[i : i + 1] = row[0][0:1]
    inverse = rows_ref[:, RANK:]
    zero = jnp.zeros((RANK, RANK), f32)
    pair = jnp.concatenate(
        [jnp.concatenate([inverse, zero], axis=1), jnp.concatenate([zero, inverse], axis=1)], axis=0
    )
    packed = jnp.concatenate([gathered[CHUNK * i : CHUNK * i + SLICE] for i in range(FRM)], axis=0)
    left = split_three(packed)
    right = split_three(pair)
    outer = jnp.concatenate(right[:2], axis=0)
    projected = dot_nt(jnp.concatenate(left[:2], axis=1), jnp.concatenate([outer, outer], axis=1))
    rest = dot_nt(jnp.concatenate([left[0], left[2]], axis=1), jnp.concatenate([right[2], right[0]], axis=1))
    projected = projected[:, :128] + (projected[:, 128:] + rest)
    projected_out[...] = projected
    subspace_out[...] = dot_nn(inverse, krylov[...], precision=highest)
    hi, lo = split_two(projected)
    gram = dot_tn(hi, hi) + (dot_tn(hi, lo) + dot_tn(lo, hi))
    gram = gram[:RANK, :RANK] + gram[RANK:, RANK:]
    gram = pack_symmetric(gram).astype(bf16)
    for i in range(PIX):
        out[i] = gram


def finish_kernel(grams, subspace, video, multiplier, projected, sparse_out, multiplier_out, out, near, rows_ref, sems):
    gram = grams[0].astype(f32)
    for i in range(1, PIX):
        gram = gram + grams[i].astype(f32)
    gram = unpack_symmetric(gram)
    rows = lax.broadcasted_iota(jnp.int32, (RANK, RANK), 0)
    cols = lax.broadcasted_iota(jnp.int32, (RANK, RANK), 1)
    eye = jnp.where(rows == cols, 1.0, 0.0).astype(f32)
    level = jnp.sum(jnp.sum(gram * eye, axis=0, keepdims=True), axis=1, keepdims=True) * (shrink_ratio / RANK)
    wide = [subspace[8 * i : 8 * i + 8] for i in range(8)]
    blocks = [[x, y[:, :128], y[:, 128:]] for x, y in zip(augment(gram + level * eye), wide)]
    for i, row in enumerate(factorize(blocks)):
        for j in range(3):
            rows_ref[i : i + 1, 128 * j : 128 * j + 128] = row[j][0:1]
    mixed = subspace[...] - level * dot_tn(rows_ref[:, RANK:128], rows_ref[:, 128:], precision=highest)
    zero = jnp.zeros((RANK, COLS), bf16)
    parts = split_two(mixed)
    weighted = [[jnp.concatenate(pair, axis=0) for pair in ((part, zero), (zero, part))] for part in parts]
    weighted[0] = [jnp.concatenate([pair, pair], axis=0) for pair in weighted[0]]

    residual_sq = jnp.zeros((8, COLS), f32)
    video_sq = jnp.zeros((8, COLS), f32)
    copies = []
    for i in range(STEPS):
        rows = slice(TILE * i, TILE * i + TILE)
        hi, lo = split_two(projected[rows])
        both = jnp.concatenate([hi, lo], axis=1)
        for h in range(2):
            low_rank = dot_nn(both, weighted[0][h]) + dot_nn(hi, weighted[1][h])
            video_full = video[h, rows].astype(f32)
            held = multiplier[h, rows]
            base = video_full - low_rank
            shifted = base + held * inverse_mu
            sparse_next = shifted - jnp.clip(shifted, -sparse_cut, sparse_cut)
            residual = base - sparse_next
            near[0, h, rows] = sparse_next
            near[1, h, rows] = held + mu_value * residual
            for j, target in enumerate((sparse_out, multiplier_out)):
                at = (h, pl.ds(TILE * i, TILE))
                copies.append(pltpu.make_async_copy(near.at[j].at[at], target.at[at], sems.at[len(copies)]))
                copies[-1].start()
            residual_sq += jnp.sum((residual * residual).reshape(TILE // 8, 8, COLS), axis=0)
            video_sq += jnp.sum((video_full * video_full).reshape(TILE // 8, 8, COLS), axis=0)
    residual_sq = jnp.sum(residual_sq, axis=0, keepdims=True)
    video_sq = jnp.sum(video_sq, axis=0, keepdims=True)
    tile = jnp.concatenate(
        [residual_sq[:, :128], residual_sq[:, 128:], video_sq[:, :128], video_sq[:, 128:]],
        axis=0,
    )
    for i in range(PIX):
        out[4 * i : 4 * i + 4] = tile
    for copy in copies:
        copy.wait()


def ratio_kernel(x, out):
    total = x[:4]
    for i in range(1, PIX):
        total = total + x[4 * i : 4 * i + 4]
    out[...] = jnp.sqrt(total[0:2] / (total[2:4] + epsilon_value))


def struct(shape, dtype=f32):
    return jax.ShapeDtypeStruct(shape, dtype)


def whole(kernel, outs, count, **kw):
    return pl.pallas_call(
        kernel,
        out_shape=outs,
        in_specs=[vmem] * count,
        out_specs=jax.tree.map(lambda _: vmem, outs),
        compiler_params=params,
        **kw,
    )


def exchange(x, axis):
    peers = FRM if axis == "frm" else PIX
    parts = (peers, 1, -1) if x.dtype == f32 else (peers, -1, 128)
    index = [[p * FRM + f for f in range(FRM)] for p in range(PIX)]
    groups = index if axis == "frm" else [list(group) for group in zip(*index)]
    return lax.all_to_all(x.reshape(parts), ("pix", "frm"), 0, 0, axis_index_groups=groups).reshape(x.shape)


def per_device(video, sparse, multiplier, start_block):
    video, sparse, multiplier = (x.reshape(2, HALF, COLS) for x in (video, sparse, multiplier))
    far = pl.BlockSpec(memory_space=pltpu.HBM)
    working, across = pl.pallas_call(
        start_kernel,
        out_shape=(struct((2, HALF, COLS), bf16), struct((HALF, 128), bf16)),
        in_specs=[far] * 4,
        out_specs=(vmem, vmem),
        scratch_shapes=[
            pltpu.VMEM((2, HALF, COLS), bf16),
            pltpu.VMEM((2, HALF, COLS), f32),
            pltpu.VMEM((2, HALF, COLS), f32),
            pltpu.VMEM((RANK, COLS), bf16),
            pltpu.SemaphoreType.DMA((3 * START_STEPS + 1,)),
        ],
        compiler_params=params,
    )(*(pltpu.with_memory_space_constraint(x, pltpu.HBM) for x in (video, sparse, multiplier, start_block.T)))

    across = exchange(across, "frm")
    across = whole(functools.partial(sum_kernel, FRM), struct((HALF, 128), bf16), 1)(across)
    across = exchange(across, "frm")

    krylov = whole(krylov_kernel, struct((128, 128)), 2)(across, working)
    krylov = exchange(krylov, "pix")
    krylov = whole(functools.partial(sum_kernel, PIX), struct((128, 128)), 1)(krylov)
    krylov = exchange(krylov, "pix")

    wide = struct((FRM * CHUNK, 128))
    krylov, projected = whole(project_kernel, (struct((RANK, COLS)), wide), 2)(krylov, working)
    projected = exchange(projected, "frm")
    projected = whole(functools.partial(sum_kernel, FRM), wide, 1)(projected)
    projected = exchange(projected, "frm")

    projected, subspace, grams = whole(
        basis_kernel,
        (struct((HALF, 128)), struct((RANK, COLS)), struct((PIX, 24, 128), bf16)),
        2,
        scratch_shapes=[pltpu.VMEM((RANK, 128), f32)],
    )(projected, krylov)
    grams = exchange(grams, "pix")

    sparse_next, multiplier_next, sums = pl.pallas_call(
        finish_kernel,
        out_shape=(struct((2, HALF, COLS)), struct((2, HALF, COLS)), struct((PIX * 4, 128))),
        in_specs=[vmem] * 5,
        out_specs=(far, far, vmem),
        scratch_shapes=[pltpu.VMEM((2, 2, HALF, COLS), f32), pltpu.VMEM((RANK, 3 * 128), f32), pltpu.SemaphoreType.DMA((4 * STEPS,))],
        compiler_params=params,
    )(grams, subspace, video, multiplier, projected)
    sums = exchange(sums, "pix")
    ratio = whole(ratio_kernel, struct((2, 128)), 1)(sums)

    shape = (ROWS, COLS)
    return sparse_next.reshape(shape), multiplier_next.reshape(shape), ratio.reshape(COLS)


def solution(mesh):
    placed = (P("pix", "frm"), P("pix", "frm"), P("pix", "frm"), P("frm", None))
    return jax.shard_map(
        per_device,
        mesh=mesh,
        in_specs=placed,
        out_specs=(P("pix", "frm"), P("pix", "frm"), P("frm")),
        check_vma=False,
    )
```

```python
import functools

import jax
import jax.numpy as jnp
from jax import lax
from jax.experimental import pallas as pl
from jax.experimental.pallas import tpu as pltpu
from jax.sharding import PartitionSpec as P

mu_value = 1.25
inverse_mu = 0.8
sparse_cut = 0.8
shrink_ratio = 0.25
epsilon_value = 1e-06

f32 = jnp.float32
bf16 = jnp.bfloat16
highest = lax.Precision.HIGHEST

FRM = 32
PIX = 16
ROWS = 1024
HALF = 512
COLS = 256
RANK = 64
START_STEPS = 2
START_TILE = HALF // START_STEPS
STEPS = 4
TILE = HALF // STEPS
SLICE = HALF // FRM
CHUNK = SLICE + 1

vmem = pl.BlockSpec(memory_space=pltpu.VMEM)
params = pltpu.CompilerParams(vmem_limit_bytes=40 * 1024 * 1024)


def dot_nt(a, b, **kw):
    return lax.dot_general(a, b, (((1,), (1,)), ((), ())), preferred_element_type=f32, **kw)


def dot_tn(a, b, **kw):
    return lax.dot_general(a, b, (((0,), (0,)), ((), ())), preferred_element_type=f32, **kw)


def dot_nn(a, b, **kw):
    return lax.dot_general(a, b, (((1,), (0,)), ((), ())), preferred_element_type=f32, **kw)


def split_two(x):
    hi = x.astype(bf16)
    return hi, (x - hi.astype(f32)).astype(bf16)


def split_three(x):
    hi = x.astype(bf16)
    rest = x - hi.astype(f32)
    mid = rest.astype(bf16)
    return hi, mid, (rest - mid.astype(f32)).astype(bf16)


def sub_iota():
    return lax.broadcasted_iota(jnp.int32, (8, 128), 0)


def lane_iota():
    return lax.broadcasted_iota(jnp.int32, (8, 128), 1)


def row_of(x, k):
    return jnp.broadcast_to(x[k : k + 1, :], (8, 128))


def column_of(x, c):
    return jnp.broadcast_to(x[:, c : c + 1], (8, 128))


def augment(a):
    blocks = []
    for b in range(8):
        eye = jnp.where(lane_iota() == sub_iota() + (8 * b + 64), 1.0, 0.0).astype(f32)
        part = a[8 * b : 8 * b + 8]
        blocks.append(jnp.where(lane_iota() < 64, jnp.concatenate([part, part], axis=1), eye))
    return blocks


def fold(block, cols, rows):
    terms = [col * row for col, row in zip(cols, rows)]
    while len(terms) > 1:
        terms = [x + y for x, y in zip(terms[::2], terms[1::2])]
    return block - terms[0]


def rows_of(x):
    return [row_of(x, j) for j in range(8)]


def invert(blocks):
    blocks = list(blocks)
    sub = sub_iota()
    for b in range(8):
        lead = blocks[b]
        cols = [column_of(lead, 8 * b + j) for j in range(8)]
        others = [i % 8 for i in range(b + 1, b + 8)]
        mults = {i: [column_of(blocks[i], 8 * b + j) for j in range(8)] for i in others}
        for k in range(8):
            inverse = 1.0 / row_of(cols[k], k)
            mult = cols[k] * inverse
            for j in range(k + 1, 8):
                row = row_of(cols[j], k)
                cols[j] = jnp.where(sub == k, row * inverse, cols[j] - mult * row)
            row = row_of(lead, k)
            lead = jnp.where(sub == k, row * inverse, lead - mult * row)
        blocks[b] = lead
        lead_rows = rows_of(lead)
        for i in others:
            blocks[i] = fold(blocks[i], mults[i], lead_rows)
    return blocks


def factorize(blocks):
    blocks = [list(block) for block in blocks]
    sub = sub_iota()
    rows = []
    cols = [column_of(blocks[0][0], j) for j in range(8)]
    for b in range(8):
        lead, last = blocks[b], b == 7
        mults = {i: [column_of(blocks[i][0], 8 * b + j) for j in range(8)] for i in range(b + 1, 8)}
        if not last:
            ahead = [column_of(blocks[b + 1][0], 8 * b + 8 + j) for j in range(8)]
            cols = cols + [column_of(lead[0], 8 * b + 8 + j) for j in range(8)]
        for k in range(8):
            lead_row = [row_of(x, k) for x in lead]
            root = lax.rsqrt(row_of(cols[k], k))
            rows.append([x * root for x in lead_row])
            inverse = root * root
            mult = cols[k] * inverse
            for j in range(k + 1, len(cols)):
                row = row_of(cols[j], k)
                cols[j] = jnp.where(sub == k, row * inverse, cols[j] - mult * row)
            lead = [jnp.where(sub == k, y * inverse, x - mult * y) for x, y in zip(lead, lead_row)]
        if last:
            break
        cols = [fold(ahead[j], mults[b + 1], rows_of(cols[8 + j])) for j in range(8)]
        lead_rows = [rows_of(x) for x in lead]
        for i in range(b + 1, 8):
            blocks[i] = [fold(x, mults[i], y) for x, y in zip(blocks[i], lead_rows)]
    return rows


def pack_symmetric(gram):
    wide = jnp.concatenate([gram[:32], gram[32:]], axis=1)
    free = (lane_iota() >= 64) & (lane_iota() < 96)
    tail = wide[24:]
    return jnp.concatenate(
        [jnp.where(free, pltpu.roll(tail, shift, 1), wide[8 * i : 8 * i + 8]) for i, shift in enumerate((64, 32, 96))],
        axis=0,
    )


def unpack_symmetric(packed):
    lane = lane_iota()
    first, second, third = (pltpu.roll(packed[8 * i : 8 * i + 8], shift, 1) for i, shift in enumerate((64, 96, 32)))
    tail = jnp.where(lane < 32, first, jnp.where(lane < 64, second, third))
    wide = jnp.concatenate([packed, tail], axis=0)
    upper = wide[:, :64]
    lower = jnp.concatenate([upper[:, 32:].T, wide[:, 96:]], axis=1)
    return jnp.concatenate([upper, lower], axis=0)


def start_kernel(video, sparse, multiplier, start, working, across, video_in, sparse_in, multiplier_in, start_in, sems):
    sources = ((video, video_in), (sparse, sparse_in), (multiplier, multiplier_in))
    copies = [pltpu.make_async_copy(start, start_in, sems.at[3 * START_STEPS])]
    for i in range(START_STEPS):
        rows = pl.ds(START_TILE * i, START_TILE)
        for j, (source, target) in enumerate(sources):
            copies.append(pltpu.make_async_copy(source.at[:, rows], target.at[:, rows], sems.at[3 * i + j]))
    for copy in copies:
        copy.start()
    copies[0].wait()
    for i in range(START_STEPS):
        rows = slice(START_TILE * i, START_TILE * i + START_TILE)
        for copy in copies[1 + 3 * i : 4 + 3 * i]:
            copy.wait()
        halves = []
        for h in range(2):
            value = video_in[h, rows].astype(f32) - sparse_in[h, rows] + multiplier_in[h, rows] * inverse_mu
            value = value.astype(bf16)
            working[h, rows] = value
            halves.append(dot_nt(value, start_in[...]))
        across[rows] = jnp.concatenate(halves, axis=1).astype(bf16)


def sum_kernel(peers, x, out):
    rows = x.shape[0] // peers
    total = x[:rows].astype(f32)
    for i in range(1, peers):
        total = total + x[rows * i : rows * i + rows].astype(f32)
    total = total.astype(out.dtype)
    for i in range(peers):
        out[rows * i : rows * i + rows] = total


def krylov_kernel(across, working, out):
    packed = across[...]
    first = dot_tn(packed, working[0])
    second = dot_tn(packed, working[1])
    krylov = first[:RANK] + second[RANK:]
    for i in range(8):
        out[8 * i : 8 * i + 8] = krylov[8 * i : 8 * i + 8, :128]
        out[RANK + 8 * i : RANK + 8 * i + 8] = krylov[8 * i : 8 * i + 8, 128:]


def project_kernel(gathered, working, krylov_out, out):
    packed = gathered[...]
    krylov = jnp.concatenate([packed[:RANK], packed[RANK:]], axis=1)
    krylov_out[...] = krylov
    zero = jnp.zeros((RANK, COLS), bf16)
    first, second, third = split_three(krylov)
    low = dot_nt(working[0], jnp.concatenate([first, zero, second, zero], axis=0))
    high = dot_nt(working[1], jnp.concatenate([zero, first, zero, second], axis=0))
    total = dot_nt(working[0], jnp.concatenate([third, zero], axis=0))
    total = total + dot_nt(working[1], jnp.concatenate([zero, third], axis=0))
    total = (total + (low[:, 128:] + high[:, 128:])) + (low[:, :128] + high[:, :128])
    gram = dot_nt(krylov, krylov, precision=highest)
    gram = jnp.concatenate([gram[:32], gram[32:]], axis=1)
    for i in range(FRM):
        at = CHUNK * i
        out[at : at + SLICE] = total[SLICE * i : SLICE * i + SLICE]
        out[at + SLICE : at + CHUNK] = gram[i : i + 1]


def basis_kernel(gathered, krylov, projected_out, subspace_out, out, rows_ref):
    gram = jnp.concatenate([gathered[CHUNK * i + SLICE : CHUNK * i + CHUNK] for i in range(FRM)], axis=0)
    gram = jnp.concatenate([gram[:, :RANK], gram[:, RANK:]], axis=0)
    for i, row in enumerate(factorize([[block] for block in augment(gram)])):
        rows_ref[i : i + 1] = row[0][0:1]
    inverse = rows_ref[:, RANK:]
    zero = jnp.zeros((RANK, RANK), f32)
    pair = jnp.concatenate(
        [jnp.concatenate([inverse, zero], axis=1), jnp.concatenate([zero, inverse], axis=1)], axis=0
    )
    packed = jnp.concatenate([gathered[CHUNK * i : CHUNK * i + SLICE] for i in range(FRM)], axis=0)
    left = split_three(packed)
    right = split_three(pair)
    outer = jnp.concatenate(right[:2], axis=0)
    projected = dot_nt(jnp.concatenate(left[:2], axis=1), jnp.concatenate([outer, outer], axis=1))
    rest = dot_nt(jnp.concatenate([left[0], left[2]], axis=1), jnp.concatenate([right[2], right[0]], axis=1))
    projected = projected[:, :128] + (projected[:, 128:] + rest)
    projected_out[...] = projected
    subspace_out[...] = dot_nn(inverse, krylov[...], precision=highest)
    hi, lo = split_two(projected)
    gram = dot_tn(hi, jnp.concatenate([hi, lo], axis=1))
    gram = gram[:RANK] + jnp.concatenate([pltpu.roll(gram[RANK:, :128], 64, 1), pltpu.roll(gram[RANK:, 128:], 64, 1)], axis=1)
    rest = gram[:, 128 : 128 + RANK]
    gram = gram[:, :RANK] + (rest + rest.T)
    gram = pack_symmetric(gram).astype(bf16)
    for i in range(PIX):
        out[i] = gram


def finish_kernel(grams, subspace, video, multiplier, projected, sparse_out, multiplier_out, out, near, rows_ref, sems):
    gram = grams[0].astype(f32)
    for i in range(1, PIX):
        gram = gram + grams[i].astype(f32)
    gram = unpack_symmetric(gram)
    rows = lax.broadcasted_iota(jnp.int32, (RANK, RANK), 0)
    cols = lax.broadcasted_iota(jnp.int32, (RANK, RANK), 1)
    eye = jnp.where(rows == cols, 1.0, 0.0).astype(f32)
    level = jnp.sum(jnp.sum(gram * eye, axis=0, keepdims=True), axis=1, keepdims=True) * (shrink_ratio / RANK)
    wide = [subspace[8 * i : 8 * i + 8] for i in range(8)]
    blocks = [[x, y[:, :128], y[:, 128:]] for x, y in zip(augment(gram + level * eye), wide)]
    for i, row in enumerate(factorize(blocks)):
        for j in range(3):
            rows_ref[i : i + 1, 128 * j : 128 * j + 128] = row[j][0:1]
    mixed = subspace[...] - level * dot_tn(rows_ref[:, RANK:128], rows_ref[:, 128:], precision=highest)
    zero = jnp.zeros((RANK, COLS), bf16)
    parts = split_two(mixed)
    weighted = [[jnp.concatenate(pair, axis=0) for pair in ((part, zero), (zero, part))] for part in parts]
    weighted[0] = [jnp.concatenate([pair, pair], axis=0) for pair in weighted[0]]

    residual_sq = jnp.zeros((8, COLS), f32)
    video_sq = jnp.zeros((8, COLS), f32)
    copies = []
    for i in range(STEPS):
        rows = slice(TILE * i, TILE * i + TILE)
        hi, lo = split_two(projected[rows])
        both = jnp.concatenate([hi, lo], axis=1)
        for h in range(2):
            low_rank = dot_nn(both, weighted[0][h]) + dot_nn(hi, weighted[1][h])
            video_full = video[h, rows].astype(f32)
            held = multiplier[h, rows]
            base = video_full - low_rank
            shifted = base + held * inverse_mu
            sparse_next = shifted - jnp.clip(shifted, -sparse_cut, sparse_cut)
            residual = base - sparse_next
            near[0, h, rows] = sparse_next
            near[1, h, rows] = held + mu_value * residual
            for j, target in enumerate((sparse_out, multiplier_out)):
                at = (h, pl.ds(TILE * i, TILE))
                copies.append(pltpu.make_async_copy(near.at[j].at[at], target.at[at], sems.at[len(copies)]))
                copies[-1].start()
            residual_sq += jnp.sum((residual * residual).reshape(TILE // 8, 8, COLS), axis=0)
            video_sq += jnp.sum((video_full * video_full).reshape(TILE // 8, 8, COLS), axis=0)
    residual_sq = jnp.sum(residual_sq, axis=0, keepdims=True)
    video_sq = jnp.sum(video_sq, axis=0, keepdims=True)
    tile = jnp.concatenate(
        [residual_sq[:, :128], residual_sq[:, 128:], video_sq[:, :128], video_sq[:, 128:]],
        axis=0,
    )
    for i in range(PIX):
        out[4 * i : 4 * i + 4] = tile
    for copy in copies:
        copy.wait()


def ratio_kernel(x, out):
    total = x[:4]
    for i in range(1, PIX):
        total = total + x[4 * i : 4 * i + 4]
    out[...] = jnp.sqrt(total[0:2] / (total[2:4] + epsilon_value))


def struct(shape, dtype=f32):
    return jax.ShapeDtypeStruct(shape, dtype)


def whole(kernel, outs, count, **kw):
    return pl.pallas_call(
        kernel,
        out_shape=outs,
        in_specs=[vmem] * count,
        out_specs=jax.tree.map(lambda _: vmem, outs),
        compiler_params=params,
        **kw,
    )


def exchange(x, axis):
    peers = FRM if axis == "frm" else PIX
    parts = (peers, 1, -1) if x.dtype == f32 else (peers, -1, 128)
    index = [[p * FRM + f for f in range(FRM)] for p in range(PIX)]
    groups = index if axis == "frm" else [list(group) for group in zip(*index)]
    return lax.all_to_all(x.reshape(parts), ("pix", "frm"), 0, 0, axis_index_groups=groups).reshape(x.shape)


def per_device(video, sparse, multiplier, start_block):
    video, sparse, multiplier = (x.reshape(2, HALF, COLS) for x in (video, sparse, multiplier))
    far = pl.BlockSpec(memory_space=pltpu.HBM)
    working, across = pl.pallas_call(
        start_kernel,
        out_shape=(struct((2, HALF, COLS), bf16), struct((HALF, 128), bf16)),
        in_specs=[far] * 4,
        out_specs=(vmem, vmem),
        scratch_shapes=[
            pltpu.VMEM((2, HALF, COLS), bf16),
            pltpu.VMEM((2, HALF, COLS), f32),
            pltpu.VMEM((2, HALF, COLS), f32),
            pltpu.VMEM((RANK, COLS), bf16),
            pltpu.SemaphoreType.DMA((3 * START_STEPS + 1,)),
        ],
        compiler_params=params,
    )(*(pltpu.with_memory_space_constraint(x, pltpu.HBM) for x in (video, sparse, multiplier, start_block.T)))

    across = exchange(across, "frm")
    across = whole(functools.partial(sum_kernel, FRM), struct((HALF, 128), bf16), 1)(across)
    across = exchange(across, "frm")

    krylov = whole(krylov_kernel, struct((128, 128)), 2)(across, working)
    krylov = exchange(krylov, "pix")
    krylov = whole(functools.partial(sum_kernel, PIX), struct((128, 128)), 1)(krylov)
    krylov = exchange(krylov, "pix")

    wide = struct((FRM * CHUNK, 128))
    krylov, projected = whole(project_kernel, (struct((RANK, COLS)), wide), 2)(krylov, working)
    projected = exchange(projected, "frm")
    projected = whole(functools.partial(sum_kernel, FRM), wide, 1)(projected)
    projected = exchange(projected, "frm")

    projected, subspace, grams = whole(
        basis_kernel,
        (struct((HALF, 128)), struct((RANK, COLS)), struct((PIX, 24, 128), bf16)),
        2,
        scratch_shapes=[pltpu.VMEM((RANK, 128), f32)],
    )(projected, krylov)
    grams = exchange(grams, "pix")

    sparse_next, multiplier_next, sums = pl.pallas_call(
        finish_kernel,
        out_shape=(struct((2, HALF, COLS)), struct((2, HALF, COLS)), struct((PIX * 4, 128))),
        in_specs=[vmem] * 5,
        out_specs=(far, far, vmem),
        scratch_shapes=[pltpu.VMEM((2, 2, HALF, COLS), f32), pltpu.VMEM((RANK, 3 * 128), f32), pltpu.SemaphoreType.DMA((4 * STEPS,))],
        compiler_params=params,
    )(grams, subspace, video, multiplier, projected)
    sums = exchange(sums, "pix")
    ratio = whole(ratio_kernel, struct((2, 128)), 1)(sums)

    shape = (ROWS, COLS)
    return sparse_next.reshape(shape), multiplier_next.reshape(shape), ratio.reshape(COLS)


def solution(mesh):
    placed = (P("pix", "frm"), P("pix", "frm"), P("pix", "frm"), P("frm", None))
    return jax.shard_map(
        per_device,
        mesh=mesh,
        in_specs=placed,
        out_specs=(P("pix", "frm"), P("pix", "frm"), P("frm")),
        check_vma=False,
    )
```

```python
import functools

import jax
import jax.numpy as jnp
from jax import lax
from jax.experimental import pallas as pl
from jax.experimental.pallas import tpu as pltpu
from jax.sharding import PartitionSpec as P

mu_value = 1.25
inverse_mu = 0.8
sparse_cut = 0.8
shrink_ratio = 0.25
epsilon_value = 1e-06

f32 = jnp.float32
bf16 = jnp.bfloat16
highest = lax.Precision.HIGHEST

FRM = 32
PIX = 16
ROWS = 1024
HALF = 512
COLS = 256
RANK = 64
START_STEPS = 2
START_TILE = HALF // START_STEPS
STEPS = 4
TILE = HALF // STEPS
SLICE = HALF // FRM
CHUNK = SLICE + 1

vmem = pl.BlockSpec(memory_space=pltpu.VMEM)
params = pltpu.CompilerParams(vmem_limit_bytes=40 * 1024 * 1024)


def dot_nt(a, b, **kw):
    return lax.dot_general(a, b, (((1,), (1,)), ((), ())), preferred_element_type=f32, **kw)


def dot_tn(a, b, **kw):
    return lax.dot_general(a, b, (((0,), (0,)), ((), ())), preferred_element_type=f32, **kw)


def dot_nn(a, b, **kw):
    return lax.dot_general(a, b, (((1,), (0,)), ((), ())), preferred_element_type=f32, **kw)


def split_two(x):
    hi = x.astype(bf16)
    return hi, (x - hi.astype(f32)).astype(bf16)


def split_three(x):
    hi = x.astype(bf16)
    rest = x - hi.astype(f32)
    mid = rest.astype(bf16)
    return hi, mid, (rest - mid.astype(f32)).astype(bf16)


def sub_iota():
    return lax.broadcasted_iota(jnp.int32, (8, 128), 0)


def lane_iota():
    return lax.broadcasted_iota(jnp.int32, (8, 128), 1)


def row_of(x, k):
    return jnp.broadcast_to(x[k : k + 1, :], (8, 128))


def column_of(x, c):
    return jnp.broadcast_to(x[:, c : c + 1], (8, 128))


def augment(a):
    blocks = []
    for b in range(8):
        eye = jnp.where(lane_iota() == sub_iota() + (8 * b + 64), 1.0, 0.0).astype(f32)
        part = a[8 * b : 8 * b + 8]
        blocks.append(jnp.where(lane_iota() < 64, jnp.concatenate([part, part], axis=1), eye))
    return blocks


def fold(block, cols, rows):
    terms = [col * row for col, row in zip(cols, rows)]
    while len(terms) > 1:
        terms = [x + y for x, y in zip(terms[::2], terms[1::2])]
    return block - terms[0]


def rows_of(x):
    return [row_of(x, j) for j in range(8)]


def invert(blocks):
    blocks = list(blocks)
    sub = sub_iota()
    for b in range(8):
        lead = blocks[b]
        cols = [column_of(lead, 8 * b + j) for j in range(8)]
        others = [i % 8 for i in range(b + 1, b + 8)]
        mults = {i: [column_of(blocks[i], 8 * b + j) for j in range(8)] for i in others}
        for k in range(8):
            inverse = 1.0 / row_of(cols[k], k)
            mult = cols[k] * inverse
            for j in range(k + 1, 8):
                row = row_of(cols[j], k)
                cols[j] = jnp.where(sub == k, row * inverse, cols[j] - mult * row)
            row = row_of(lead, k)
            lead = jnp.where(sub == k, row * inverse, lead - mult * row)
        blocks[b] = lead
        lead_rows = rows_of(lead)
        for i in others:
            blocks[i] = fold(blocks[i], mults[i], lead_rows)
    return blocks


def factorize(blocks):
    blocks = [list(block) for block in blocks]
    sub = sub_iota()
    rows = []
    cols = [column_of(blocks[0][0], j) for j in range(8)]
    for b in range(8):
        lead, last = blocks[b], b == 7
        mults = {i: [column_of(blocks[i][0], 8 * b + j) for j in range(8)] for i in range(b + 1, 8)}
        if not last:
            ahead = [column_of(blocks[b + 1][0], 8 * b + 8 + j) for j in range(8)]
            cols = cols + [column_of(lead[0], 8 * b + 8 + j) for j in range(8)]
        for k in range(8):
            lead_row = [row_of(x, k) for x in lead]
            root = lax.rsqrt(row_of(cols[k], k))
            rows.append([x * root for x in lead_row])
            inverse = root * root
            mult = cols[k] * inverse
            for j in range(k + 1, len(cols)):
                row = row_of(cols[j], k)
                cols[j] = jnp.where(sub == k, row * inverse, cols[j] - mult * row)
            lead = [jnp.where(sub == k, y * inverse, x - mult * y) for x, y in zip(lead, lead_row)]
        if last:
            break
        cols = [fold(ahead[j], mults[b + 1], rows_of(cols[8 + j])) for j in range(8)]
        lead_rows = [rows_of(x) for x in lead]
        for i in range(b + 1, 8):
            blocks[i] = [fold(x, mults[i], y) for x, y in zip(blocks[i], lead_rows)]
    return rows


def pack_symmetric(gram):
    wide = jnp.concatenate([gram[:32], gram[32:]], axis=1)
    free = (lane_iota() >= 64) & (lane_iota() < 96)
    tail = wide[24:]
    return jnp.concatenate(
        [jnp.where(free, pltpu.roll(tail, shift, 1), wide[8 * i : 8 * i + 8]) for i, shift in enumerate((64, 32, 96))],
        axis=0,
    )


def unpack_symmetric(packed):
    lane = lane_iota()
    first, second, third = (pltpu.roll(packed[8 * i : 8 * i + 8], shift, 1) for i, shift in enumerate((64, 96, 32)))
    tail = jnp.where(lane < 32, first, jnp.where(lane < 64, second, third))
    wide = jnp.concatenate([packed, tail], axis=0)
    upper = wide[:, :64]
    lower = jnp.concatenate([upper[:, 32:].T, wide[:, 96:]], axis=1)
    row = lax.broadcasted_iota(jnp.int32, (32, 128), 0)
    lane = lax.broadcasted_iota(jnp.int32, (32, 128), 1)
    diagonal = jnp.where((lane == row) | (lane == row + 96), wide, 0.0)
    trace = jnp.sum(jnp.sum(diagonal, axis=0, keepdims=True), axis=1, keepdims=True)
    return jnp.concatenate([upper, lower], axis=0), trace


def start_kernel(video, sparse, multiplier, start, working, across, video_in, sparse_in, multiplier_in, start_in, sems):
    sources = ((video, video_in), (sparse, sparse_in), (multiplier, multiplier_in))
    copies = [pltpu.make_async_copy(start, start_in, sems.at[3 * START_STEPS])]
    for i in range(START_STEPS):
        rows = pl.ds(START_TILE * i, START_TILE)
        for j, (source, target) in enumerate(sources):
            copies.append(pltpu.make_async_copy(source.at[:, rows], target.at[:, rows], sems.at[3 * i + j]))
    for copy in copies:
        copy.start()
    copies[0].wait()
    for i in range(START_STEPS):
        rows = slice(START_TILE * i, START_TILE * i + START_TILE)
        for copy in copies[1 + 3 * i : 4 + 3 * i]:
            copy.wait()
        halves = []
        for h in range(2):
            value = video_in[h, rows].astype(f32) - sparse_in[h, rows] + multiplier_in[h, rows] * inverse_mu
            value = value.astype(bf16)
            working[h, rows] = value
            halves.append(dot_nt(value, start_in[...]))
        across[rows] = jnp.concatenate(halves, axis=1).astype(bf16)


def sum_kernel(peers, x, out):
    rows = x.shape[0] // peers
    total = x[:rows].astype(f32)
    for i in range(1, peers):
        total = total + x[rows * i : rows * i + rows].astype(f32)
    total = total.astype(out.dtype)
    for i in range(peers):
        out[rows * i : rows * i + rows] = total


def krylov_kernel(across, working, out):
    packed = across[...]
    first = dot_tn(packed, working[0])
    second = dot_tn(packed, working[1])
    krylov = first[:RANK] + second[RANK:]
    for i in range(8):
        out[8 * i : 8 * i + 8] = krylov[8 * i : 8 * i + 8, :128]
        out[RANK + 8 * i : RANK + 8 * i + 8] = krylov[8 * i : 8 * i + 8, 128:]


def project_kernel(gathered, working, krylov_out, out):
    packed = gathered[...]
    krylov = jnp.concatenate([packed[:RANK], packed[RANK:]], axis=1)
    krylov_out[...] = krylov
    zero = jnp.zeros((RANK, COLS), bf16)
    first, second, third = split_three(krylov)
    low = dot_nt(working[0], jnp.concatenate([first, zero, second, zero], axis=0))
    high = dot_nt(working[1], jnp.concatenate([zero, first, zero, second], axis=0))
    total = dot_nt(working[0], jnp.concatenate([third, zero], axis=0))
    total = total + dot_nt(working[1], jnp.concatenate([zero, third], axis=0))
    total = (total + (low[:, 128:] + high[:, 128:])) + (low[:, :128] + high[:, :128])
    gram = dot_nt(krylov, krylov, precision=highest)
    gram = jnp.concatenate([gram[:32], gram[32:]], axis=1)
    for i in range(FRM):
        at = CHUNK * i
        out[at : at + SLICE] = total[SLICE * i : SLICE * i + SLICE]
        out[at + SLICE : at + CHUNK] = gram[i : i + 1]


def basis_kernel(gathered, krylov, projected_out, subspace_out, out, rows_ref):
    gram = jnp.concatenate([gathered[CHUNK * i + SLICE : CHUNK * i + CHUNK] for i in range(FRM)], axis=0)
    gram = jnp.concatenate([gram[:, :RANK], gram[:, RANK:]], axis=0)
    for i, row in enumerate(factorize([[block] for block in augment(gram)])):
        rows_ref[i : i + 1] = row[0][0:1]
    inverse = rows_ref[:, RANK:]
    zero = jnp.zeros((RANK, RANK), f32)
    pair = jnp.concatenate(
        [jnp.concatenate([inverse, zero], axis=1), jnp.concatenate([zero, inverse], axis=1)], axis=0
    )
    packed = jnp.concatenate([gathered[CHUNK * i : CHUNK * i + SLICE] for i in range(FRM)], axis=0)
    left = split_three(packed)
    right = split_three(pair)
    outer = jnp.concatenate(right[:2], axis=0)
    projected = dot_nt(jnp.concatenate(left[:2], axis=1), jnp.concatenate([outer, outer], axis=1))
    rest = dot_nt(jnp.concatenate([left[0], left[2]], axis=1), jnp.concatenate([right[2], right[0]], axis=1))
    projected = projected[:, :128] + (projected[:, 128:] + rest)
    projected_out[...] = projected
    subspace_out[...] = dot_nn(inverse, krylov[...], precision=highest)
    hi, lo = split_two(projected)
    gram = dot_tn(hi, hi) + (dot_tn(hi, lo) + dot_tn(lo, hi))
    gram = gram[:RANK, :RANK] + gram[RANK:, RANK:]
    gram = pack_symmetric(gram).astype(bf16)
    for i in range(PIX):
        out[i] = gram


def finish_kernel(grams, subspace, video, multiplier, projected, sparse_out, multiplier_out, out, near, rows_ref, sems):
    gram = grams[0].astype(f32)
    for i in range(1, PIX):
        gram = gram + grams[i].astype(f32)
    gram, trace = unpack_symmetric(gram)
    rows = lax.broadcasted_iota(jnp.int32, (RANK, RANK), 0)
    cols = lax.broadcasted_iota(jnp.int32, (RANK, RANK), 1)
    eye = jnp.where(rows == cols, 1.0, 0.0).astype(f32)
    level = trace * (shrink_ratio / RANK)
    wide = [subspace[8 * i : 8 * i + 8] for i in range(8)]
    blocks = [[x, y[:, :128], y[:, 128:]] for x, y in zip(augment(gram + level * eye), wide)]
    for i, row in enumerate(factorize(blocks)):
        for j in range(3):
            rows_ref[i : i + 1, 128 * j : 128 * j + 128] = row[j][0:1]
    mixed = subspace[...] - level * dot_tn(rows_ref[:, RANK:128], rows_ref[:, 128:], precision=highest)
    zero = jnp.zeros((RANK, COLS), bf16)
    parts = split_two(mixed)
    weighted = [[jnp.concatenate(pair, axis=0) for pair in ((part, zero), (zero, part))] for part in parts]
    weighted[0] = [jnp.concatenate([pair, pair], axis=0) for pair in weighted[0]]

    residual_sq = jnp.zeros((8, COLS), f32)
    video_sq = jnp.zeros((8, COLS), f32)
    copies = []
    for i in range(STEPS):
        rows = slice(TILE * i, TILE * i + TILE)
        hi, lo = split_two(projected[rows])
        both = jnp.concatenate([hi, lo], axis=1)
        for h in range(2):
            low_rank = dot_nn(both, weighted[0][h]) + dot_nn(hi, weighted[1][h])
            video_full = video[h, rows].astype(f32)
            held = multiplier[h, rows]
            base = video_full - low_rank
            shifted = base + held * inverse_mu
            sparse_next = shifted - jnp.clip(shifted, -sparse_cut, sparse_cut)
            residual = base - sparse_next
            near[0, h, rows] = sparse_next
            near[1, h, rows] = held + mu_value * residual
            for j, target in enumerate((sparse_out, multiplier_out)):
                at = (h, pl.ds(TILE * i, TILE))
                copies.append(pltpu.make_async_copy(near.at[j].at[at], target.at[at], sems.at[len(copies)]))
                copies[-1].start()
            residual_sq += jnp.sum((residual * residual).reshape(TILE // 8, 8, COLS), axis=0)
            video_sq += jnp.sum((video_full * video_full).reshape(TILE // 8, 8, COLS), axis=0)
    residual_sq = jnp.sum(residual_sq, axis=0, keepdims=True)
    video_sq = jnp.sum(video_sq, axis=0, keepdims=True)
    tile = jnp.concatenate(
        [residual_sq[:, :128], residual_sq[:, 128:], video_sq[:, :128], video_sq[:, 128:]],
        axis=0,
    )
    for i in range(PIX):
        out[4 * i : 4 * i + 4] = tile
    for copy in copies:
        copy.wait()


def ratio_kernel(x, out):
    total = x[:4]
    for i in range(1, PIX):
        total = total + x[4 * i : 4 * i + 4]
    out[...] = jnp.sqrt(total[0:2] / (total[2:4] + epsilon_value))


def struct(shape, dtype=f32):
    return jax.ShapeDtypeStruct(shape, dtype)


def whole(kernel, outs, count, **kw):
    return pl.pallas_call(
        kernel,
        out_shape=outs,
        in_specs=[vmem] * count,
        out_specs=jax.tree.map(lambda _: vmem, outs),
        compiler_params=params,
        **kw,
    )


def exchange(x, axis):
    peers = FRM if axis == "frm" else PIX
    parts = (peers, 1, -1) if x.dtype == f32 else (peers, -1, 128)
    index = [[p * FRM + f for f in range(FRM)] for p in range(PIX)]
    groups = index if axis == "frm" else [list(group) for group in zip(*index)]
    return lax.all_to_all(x.reshape(parts), ("pix", "frm"), 0, 0, axis_index_groups=groups).reshape(x.shape)


def per_device(video, sparse, multiplier, start_block):
    video, sparse, multiplier = (x.reshape(2, HALF, COLS) for x in (video, sparse, multiplier))
    far = pl.BlockSpec(memory_space=pltpu.HBM)
    working, across = pl.pallas_call(
        start_kernel,
        out_shape=(struct((2, HALF, COLS), bf16), struct((HALF, 128), bf16)),
        in_specs=[far] * 4,
        out_specs=(vmem, vmem),
        scratch_shapes=[
            pltpu.VMEM((2, HALF, COLS), bf16),
            pltpu.VMEM((2, HALF, COLS), f32),
            pltpu.VMEM((2, HALF, COLS), f32),
            pltpu.VMEM((RANK, COLS), bf16),
            pltpu.SemaphoreType.DMA((3 * START_STEPS + 1,)),
        ],
        compiler_params=params,
    )(*(pltpu.with_memory_space_constraint(x, pltpu.HBM) for x in (video, sparse, multiplier, start_block.T)))

    across = exchange(across, "frm")
    across = whole(functools.partial(sum_kernel, FRM), struct((HALF, 128), bf16), 1)(across)
    across = exchange(across, "frm")

    krylov = whole(krylov_kernel, struct((128, 128)), 2)(across, working)
    krylov = exchange(krylov, "pix")
    krylov = whole(functools.partial(sum_kernel, PIX), struct((128, 128)), 1)(krylov)
    krylov = exchange(krylov, "pix")

    wide = struct((FRM * CHUNK, 128))
    krylov, projected = whole(project_kernel, (struct((RANK, COLS)), wide), 2)(krylov, working)
    projected = exchange(projected, "frm")
    projected = whole(functools.partial(sum_kernel, FRM), wide, 1)(projected)
    projected = exchange(projected, "frm")

    projected, subspace, grams = whole(
        basis_kernel,
        (struct((HALF, 128)), struct((RANK, COLS)), struct((PIX, 24, 128), bf16)),
        2,
        scratch_shapes=[pltpu.VMEM((RANK, 128), f32)],
    )(projected, krylov)
    grams = exchange(grams, "pix")

    sparse_next, multiplier_next, sums = pl.pallas_call(
        finish_kernel,
        out_shape=(struct((2, HALF, COLS)), struct((2, HALF, COLS)), struct((PIX * 4, 128))),
        in_specs=[vmem] * 5,
        out_specs=(far, far, vmem),
        scratch_shapes=[pltpu.VMEM((2, 2, HALF, COLS), f32), pltpu.VMEM((RANK, 3 * 128), f32), pltpu.SemaphoreType.DMA((4 * STEPS,))],
        compiler_params=params,
    )(grams, subspace, video, multiplier, projected)
    sums = exchange(sums, "pix")
    ratio = whole(ratio_kernel, struct((2, 128)), 1)(sums)

    shape = (ROWS, COLS)
    return sparse_next.reshape(shape), multiplier_next.reshape(shape), ratio.reshape(COLS)


def solution(mesh):
    placed = (P("pix", "frm"), P("pix", "frm"), P("pix", "frm"), P("frm", None))
    return jax.shard_map(
        per_device,
        mesh=mesh,
        in_specs=placed,
        out_specs=(P("pix", "frm"), P("pix", "frm"), P("frm")),
        check_vma=False,
    )
```
